32 devices in a mesh: dp: 8 (over y, x, core), src: 4 (over z).
Axes of the slice: x: 2, y: 2, z: 4, core: 2. Of those that a mesh axis runs over, the one named last changes fastest.
Arguments:
- src_tok: bfloat16 [8, 1024, 512], P('dp', 'src'), may hold values from -6 to 6
- src_ids: int32 [8, 1024], P('dp'), may hold values from 0 to 7, as said below
- tgt_tok: bfloat16 [8, 1024, 512], P('dp'), may hold values from -6 to 6
- tgt_ids: int32 [8, 1024], P('dp'), may hold values from 0 to 7, as said below
- out_grad: bfloat16 [8, 1024, 512], P('dp'), may hold values from -6 to 6
- enc_attn_in: bfloat16 [512, 1536], replicated, may hold values from -0.25 to 0.25
- enc_attn_out: bfloat16 [512, 512], replicated, may hold values from -4 to 4
- enc_ffn_in: bfloat16 [512, 2048], replicated, may hold values from -0.25 to 0.25
- enc_ffn_out: bfloat16 [2048, 512], replicated, may hold values from -0.125 to 0.125
- enc_gains: float32 [2, 512], replicated, may hold values from 0.25 to 1.75
- enc_biases: float32 [2, 512], replicated, may hold values from -3 to 3
- dec_self_in: bfloat16 [512, 1536], replicated, may hold values from -0.25 to 0.25
- dec_self_out: bfloat16 [512, 512], replicated, may hold values from -4 to 4
- dec_cross_q: bfloat16 [512, 512], replicated, may hold values from -0.25 to 0.25
- dec_cross_kv: bfloat16 [512, 1024], replicated, may hold values from -0.25 to 0.25
- dec_cross_out: bfloat16 [512, 512], replicated, may hold values from -4 to 4
- dec_ffn_in: bfloat16 [512, 2048], replicated, may hold values from -0.25 to 0.25
- dec_ffn_out: bfloat16 [2048, 512], replicated, may hold values from -0.125 to 0.125
- dec_gains: float32 [3, 512], replicated, may hold values from 0.25 to 1.75
- dec_biases: float32 [3, 512], replicated, may hold values from -3 to 3
Outputs:
- dec_out: bfloat16 [8, 1024, 512], P('dp')
- src_grad: float32 [8, 1024, 512], P('dp', 'src')
- tgt_grad: float32 [8, 1024, 512], P('dp')
- grad_enc_attn_in: float32 [512, 1536], P('dp')
- grad_enc_attn_out: float32 [512, 512], P('dp')
- grad_enc_ffn_in: float32 [512, 2048], P('dp')
- grad_enc_ffn_out: float32 [2048, 512], P('dp')
- grad_enc_gains: float32 [2, 512], P(None, 'dp')
- grad_enc_biases: float32 [2, 512], P(None, 'dp')
- grad_dec_self_in: float32 [512, 1536], P('dp')
- grad_dec_self_out: float32 [512, 512], P('dp')
- grad_dec_cross_q: float32 [512, 512], P('dp')
- grad_dec_cross_kv: float32 [512, 1024], P('dp')
- grad_dec_cross_out: float32 [512, 512], P('dp')
- grad_dec_ffn_in: float32 [512, 2048], P('dp')
- grad_dec_ffn_out: float32 [2048, 512], P('dp')
- grad_dec_gains: float32 [3, 512], P(None, 'dp')
- grad_dec_biases: float32 [3, 512], P(None, 'dp')
The draws below stay inside these ranges and needn't reach their ends.
Inputs may be any that keep to these rules, and one draw needn't show every extreme that they name: `src_ids`: each row holds 8 documents numbered from 0 in order of position, every one non-empty in source and in target; target document k of a row is translated from source document k of that row. `tgt_ids`: as for src_ids, with the same numbering of documents in each row.
All inputs are finite; a program needn't handle non-finite values.
Results may differ from the reference program's by a relative error of at most 0.02.
Values may be sent and summed in bfloat16 or wider, within the bound.
No kernel may reach another device: no remote copies, remote signals or barrier semaphores. Data moves between devices by JAX's collectives and lax.ppermute only.
A program may use at most 192 MiB of HBM per device.

```python
import jax
import jax.numpy as jnp
from jax import lax

D = 512
HEADS = 8
HEAD_DIM = 64
FF = 2048
LEN = 1024
SEGS = 8
ROWS = 8


def long_slot(key):
    return jax.random.randint(jax.random.fold_in(key, 5), (ROWS, 1), 0, SEGS)


def segment_ids(key, chosen):
    short_limit = (LEN // 8 - 1) // (SEGS - 1)
    lengths = jax.random.randint(key, (ROWS, SEGS), 1, short_limit + 1)
    numbers = jnp.arange(SEGS)[None, :]
    lengths = jnp.where(numbers == chosen, 0, lengths)
    lengths = jnp.where(numbers == chosen, LEN - jnp.sum(lengths, axis=1, keepdims=True), lengths)
    boundary = jnp.cumsum(lengths, axis=1)
    places = jnp.arange(LEN)
    passed = places[None, :, None] >= boundary[:, None, :SEGS - 1]
    return jnp.sum(passed.astype(jnp.int32), axis=2).astype(jnp.int32)


def draw_src_ids(key, part):
    chosen = long_slot(key)
    key = jax.random.fold_in(key, 21)
    return segment_ids(key, chosen)


def draw_tgt_ids(key, part):
    chosen = long_slot(key)
    key = jax.random.fold_in(key, 22)
    return segment_ids(key, chosen)


def levels(stream_key, shape, shards, least, high):
    level = 1.0
    for axis_at, shards_of in shards:
        heights = jax.random.uniform(jax.random.fold_in(jax.random.fold_in(stream_key, 6), axis_at), (shards_of,), jnp.float32, least / len(shards), high / len(shards))
        level = level * jnp.repeat(jnp.exp(heights), shape[axis_at] // shards_of).reshape((-1,) + (1,) * (len(shape) - 1 - axis_at))
    return level


def scatter_about(key, shape, scale, bound, pieces=(), held_as=jnp.bfloat16):
    level = levels(key, shape, pieces, -0.22, 0.18) if pieces else 1.0
    values = jax.random.normal(key, shape, jnp.float32) * scale * level
    return jnp.minimum(jnp.maximum(values, -bound), bound).astype(held_as)


def setup_inputs(seed: int = 0) -> dict:
    keys = jax.random.split(jax.random.key(seed), 21)
    return {
        "src_tok": scatter_about(keys[0], (ROWS, LEN, D), 1.0, 6.0, ((0, 8), (1, 4))),
        "src_ids": draw_src_ids(jax.random.fold_in(keys[20], 71), 0),
        "tgt_tok": scatter_about(keys[2], (ROWS, LEN, D), 1.0, 6.0, ((0, 8),)),
        "tgt_ids": draw_tgt_ids(jax.random.fold_in(keys[20], 71), 0),
        "out_grad": scatter_about(keys[4], (ROWS, LEN, D), 1.0, 6.0, ((0, 8),)),
        "enc_attn_in": scatter_about(keys[5], (D, 3 * D), D ** -0.5, 0.25),
        "enc_attn_out": scatter_about(keys[6], (D, D), (max(4 * D // LEN, 1)) ** -0.5, 4.0),
        "enc_ffn_in": scatter_about(keys[7], (D, FF), D ** -0.5, 0.25),
        "enc_ffn_out": scatter_about(keys[8], (FF, D), FF ** -0.5, 0.125),
        "enc_gains": jnp.clip(1.0 + 0.15 * jax.random.normal(keys[9], (2, D), jnp.float32), 0.25, 1.75),
        "enc_biases": scatter_about(keys[10], (2, D), 0.5, 3.0, (), jnp.float32),
        "dec_self_in": scatter_about(keys[11], (D, 3 * D), D ** -0.5, 0.25),
        "dec_self_out": scatter_about(keys[12], (D, D), (max(4 * D // LEN, 1)) ** -0.5, 4.0),
        "dec_cross_q": scatter_about(keys[13], (D, D), D ** -0.5, 0.25),
        "dec_cross_kv": scatter_about(keys[14], (D, 2 * D), D ** -0.5, 0.25),
        "dec_cross_out": scatter_about(keys[15], (D, D), (max(4 * D // LEN, 1)) ** -0.5, 4.0),
        "dec_ffn_in": scatter_about(keys[16], (D, FF), D ** -0.5, 0.25),
        "dec_ffn_out": scatter_about(keys[17], (FF, D), FF ** -0.5, 0.125),
        "dec_gains": jnp.clip(1.0 + 0.15 * jax.random.normal(keys[18], (3, D), jnp.float32), 0.25, 1.75),
        "dec_biases": scatter_about(keys[19], (3, D), 0.5, 3.0, (), jnp.float32),
    }


@jax.custom_vjp
def low(v):
    return lax.optimization_barrier(v.astype(jnp.bfloat16)).astype(jnp.float32)

@jax.custom_vjp
def low_back(v):
    return v

def low_keep(v):
    return (low(v), None)

def low_pass(kept, grad):
    return (grad,)

def back_keep(v):
    return (v, None)

def back_low(kept, grad):
    return (low(grad),)
low.defvjp(low_keep, low_pass)
low_back.defvjp(back_keep, back_low)
EPS = 1e-05
NEGATIVE = -1e+30

def matmul(former, latter):
    return jnp.dot(former, latter, precision=lax.Precision.HIGHEST, preferred_element_type=jnp.float32)

def both_ways(tensor):
    return low(low_back(tensor))

def layer_norm(tensor, gain, bias):
    centred = tensor - lax.optimization_barrier(jnp.mean(tensor, axis=-1, keepdims=True))
    inverse = lax.rsqrt(lax.optimization_barrier(jnp.mean(centred * centred, axis=-1, keepdims=True)) + EPS)
    return centred * inverse * gain + bias

def attend(queries, key_rows, value_rows, allowed):
    count_q = queries.shape[0]
    count_k = key_rows.shape[0]
    query_heads = queries.reshape(count_q, HEADS, HEAD_DIM)
    key_heads = key_rows.reshape(count_k, HEADS, HEAD_DIM)
    value_heads = value_rows.reshape(count_k, HEADS, HEAD_DIM)
    raw_scores = jnp.einsum('qhd,khd->hqk', query_heads, key_heads, precision=lax.Precision.HIGHEST)
    scores = jnp.where(allowed[None], low_back(raw_scores) * HEAD_DIM ** (-0.5), NEGATIVE)
    maximum = lax.optimization_barrier(jnp.max(scores, axis=-1, keepdims=True))
    exponent = jnp.where(allowed[None], jnp.exp(scores - maximum), 0.0)
    shares = exponent / lax.optimization_barrier(jnp.sum(exponent, axis=-1, keepdims=True))
    mixed = jnp.einsum('hqk,khd->qhd', low(shares), value_heads, precision=lax.Precision.HIGHEST)
    return mixed.reshape(count_q, HEADS * HEAD_DIM)

def self_part(tensor, weight_in, weight_out, allowed):
    projected = both_ways(matmul(low(tensor), weight_in))
    mixed = both_ways(attend(projected[:, :D], projected[:, D:2 * D], projected[:, 2 * D:], allowed))
    return low_back(matmul(mixed, weight_out))

def feed_forward(tensor, weight_in, weight_out):
    pre_activation = low_back(matmul(low(tensor), weight_in))
    hidden = low(jax.nn.silu(pre_activation))
    return low_back(matmul(hidden, weight_out))

def both_layers(weights, source, target, source_ids, target_ids):
    enc_attn_in, enc_attn_out, enc_ffn_in, enc_ffn_out, enc_gains, enc_biases, dec_self_in, dec_self_out, dec_cross_q, dec_cross_kv, dec_cross_out, dec_ffn_in, dec_ffn_out, dec_gains, dec_biases = weights
    source_allow = source_ids[:, None] == source_ids[None, :]
    first_enc = layer_norm(source + self_part(source, enc_attn_in, enc_attn_out, source_allow), enc_gains[0], enc_biases[0])
    memory = layer_norm(first_enc + feed_forward(first_enc, enc_ffn_in, enc_ffn_out), enc_gains[1], enc_biases[1])
    places = jnp.arange(target.shape[0])
    target_allow = (target_ids[:, None] == target_ids[None, :]) & (places[None, :] <= places[:, None])
    first_dec = layer_norm(target + self_part(target, dec_self_in, dec_self_out, target_allow), dec_gains[0], dec_biases[0])
    cross_queries = both_ways(matmul(low(first_dec), dec_cross_q))
    cross_pairs = both_ways(matmul(low(memory), dec_cross_kv))
    cross_allow = target_ids[:, None] == source_ids[None, :]
    cross_mixed = both_ways(attend(cross_queries, cross_pairs[:, :D], cross_pairs[:, D:], cross_allow))
    second_dec = layer_norm(first_dec + low_back(matmul(cross_mixed, dec_cross_out)), dec_gains[1], dec_biases[1])
    return layer_norm(second_dec + feed_forward(second_dec, dec_ffn_in, dec_ffn_out), dec_gains[2], dec_biases[2])

def add_trees(former, latter):
    return former + latter

def reference(src_tok, src_ids, tgt_tok, tgt_ids, out_grad, enc_attn_in, enc_attn_out, enc_ffn_in, enc_ffn_out, enc_gains, enc_biases, dec_self_in, dec_self_out, dec_cross_q, dec_cross_kv, dec_cross_out, dec_ffn_in, dec_ffn_out, dec_gains, dec_biases):
    params = (enc_attn_in.astype(jnp.float32), enc_attn_out.astype(jnp.float32), enc_ffn_in.astype(jnp.float32), enc_ffn_out.astype(jnp.float32), enc_gains.astype(jnp.float32), enc_biases.astype(jnp.float32), dec_self_in.astype(jnp.float32), dec_self_out.astype(jnp.float32), dec_cross_q.astype(jnp.float32), dec_cross_kv.astype(jnp.float32), dec_cross_out.astype(jnp.float32), dec_ffn_in.astype(jnp.float32), dec_ffn_out.astype(jnp.float32), dec_gains.astype(jnp.float32), dec_biases.astype(jnp.float32))

    def one_row(totals, row_data):
        source, target, source_ids, target_ids, cotangent = row_data

        def forward_row(weights, source_rows, target_rows):
            return both_layers(weights, source_rows, target_rows, source_ids, target_ids)
        output, pull_back = jax.vjp(forward_row, params, source, target)
        grads, source_grad, target_grad = pull_back(cotangent)
        totals = jax.tree.map(add_trees, totals, grads)
        return (totals, (output.astype(jnp.bfloat16), source_grad, target_grad))
    zeros = jax.tree.map(jnp.zeros_like, params)
    totals, results = lax.scan(one_row, zeros, (src_tok.astype(jnp.float32), tgt_tok.astype(jnp.float32), src_ids, tgt_ids, out_grad.astype(jnp.float32)))
    return (results[0], results[1], results[2], totals[0], totals[1], totals[2], totals[3], totals[4], totals[5], totals[6], totals[7], totals[8], totals[9], totals[10], totals[11], totals[12], totals[13], totals[14])
```

```python
import jax
import jax.numpy as jnp
from jax import lax
from jax.experimental import pallas as pl
from jax.experimental.pallas import tpu as pltpu
from jax.sharding import PartitionSpec as P

HEAD_DIM = 64
PAIR = 2 * HEAD_DIM
EPS = 1e-05
NEGATIVE = -1e30
BF = jnp.bfloat16
F32 = jnp.float32
BLOCK = 256
VECTOR_ROWS = 16
ID_ROWS = 16


def dot(former, latter, dims):
    return lax.dot_general(former, latter, (dims, ((), ())), preferred_element_type=F32)


def nn(former, latter):
    return dot(former, latter, ((1,), (0,)))


def nt(former, latter):
    return dot(former, latter, ((1,), (1,)))


def tn(former, latter):
    return dot(former, latter, ((0,), (0,)))


def norm(v):
    centred = v - jnp.mean(v, axis=-1, keepdims=True)
    inverse = lax.rsqrt(jnp.mean(centred * centred, axis=-1, keepdims=True) + EPS)
    return centred * inverse, inverse


def norm_back(du, normed, inverse, gain):
    gain_grad = jnp.sum(du * normed, axis=0, keepdims=True)
    bias_grad = jnp.sum(du, axis=0, keepdims=True)
    scaled = du * gain
    mean = jnp.mean(scaled, axis=-1, keepdims=True)
    slope = jnp.mean(scaled * normed, axis=-1, keepdims=True)
    return inverse * (scaled - mean - normed * slope), gain_grad, bias_grad


def head_halves(pair, scale):
    wide = pair.astype(F32) * scale
    first = lax.broadcasted_iota(jnp.int32, wide.shape, 1) < HEAD_DIM
    return [jnp.where(first, wide, 0.0).astype(BF), jnp.where(first, 0.0, wide).astype(BF)]


def pair_columns(pair, offset=0):
    return pl.ds(pl.multiple_of(pair * PAIR + offset, PAIR), PAIR)


def mask_bias(key_ids, query_ids):
    return jnp.where(key_ids == query_ids, 0.0, NEGATIVE)


def pair_forward(q, k, v, bias):
    queries = head_halves(q, HEAD_DIM**-0.5)
    values = v.T
    mixed, stats = [], []
    for head in range(2):
        s = nt(k, queries[head]) + bias
        maximum = jnp.max(s, axis=0, keepdims=True)
        e = jnp.exp(s - maximum)
        total = jnp.sum(e, axis=0, keepdims=True)
        o = nn(values[head * HEAD_DIM : (head + 1) * HEAD_DIM], e.astype(BF))
        mixed.append(o * (1.0 / total))
        stats.append(maximum + jnp.log(total))
    return jnp.concatenate(mixed, axis=0).T, jnp.concatenate(stats, axis=0)


def pair_delta(o, grad):
    product = (o * grad.astype(F32)).T
    return (
        jnp.sum(product[:HEAD_DIM], axis=0, keepdims=True),
        jnp.sum(product[HEAD_DIM:], axis=0, keepdims=True),
    )


def block_backward(qs, gs, k, v, keys, bias, stats, deltas):
    dq, dk, dv = [], None, None
    for head in range(2):
        s = nt(k, qs[head]) + bias
        p = jnp.exp(s - stats[head : head + 1])
        ds = (p * (nt(v, gs[head]) - deltas[head])).astype(BF)
        p = p.astype(BF)
        dq.append(nn(keys[head * HEAD_DIM : (head + 1) * HEAD_DIM], ds))
        dk_term, dv_term = nn(ds, qs[head]), nn(p, gs[head])
        dk = dk_term if dk is None else dk + dk_term
        dv = dv_term if dv is None else dv + dv_term
    return jnp.concatenate(dq, axis=0), dk, dv


def cross_backward(q_ref, kv_ref, o_ref, g_ref, bias_ref, stats_ref, dq_ref, dkv_ref):
    features = q_ref.shape[1]
    keys_count = kv_ref.shape[0]

    def one_pair(pair, carry):
        columns = pair_columns(pair)
        value_columns = pair_columns(pair, features)
        q, g = q_ref[:, columns], g_ref[:, columns]
        qs = head_halves(q, HEAD_DIM**-0.5)
        gs = head_halves(g, 1.0)
        deltas = pair_delta(o_ref[:, columns], g)
        stats = stats_ref[pair]
        total = None
        for first in range(0, keys_count, BLOCK):
            rows = slice(first, first + BLOCK)
            k = kv_ref[rows, columns]
            term, dk, dv = block_backward(
                qs, gs, k, kv_ref[rows, value_columns], k.T, bias_ref[rows, :], stats, deltas
            )
            dkv_ref[rows, columns] = dk.astype(BF)
            dkv_ref[rows, value_columns] = dv.astype(BF)
            total = term if total is None else total + term
        dq_ref[:, columns] = (total.T * HEAD_DIM**-0.5).astype(BF)
        return carry

    lax.fori_loop(0, features // PAIR, one_pair, 0)


def emit(me_dp, product, former, latter, send, keep, offset):
    devices = 2 * send.shape[0]
    width = product.shape[2]
    height = former.shape[1]
    rows = height // devices
    for first in range(0, latter.shape[1], width):
        term = tn(former, latter[:, first : first + width]).astype(BF)
        product[:, :rows, :] = term.reshape(devices, rows, width)
        for slot in range(devices):
            target = send if slot % 2 else keep
            target[slot // 2, offset : offset + rows, :] = product[
                jnp.bitwise_xor(me_dp, slot), :rows, :
            ]
        offset += rows
    return offset


def sigmoid(v):
    return 1.0 / (1.0 + jnp.exp(-v))


def silu_parts(pre):
    squashed = sigmoid(pre)
    return pre * squashed, squashed * (1.0 + pre * (1.0 - squashed))


def blocks_of(refs, height, own):
    found = []
    for ref in refs:
        for first in range(0, ref.shape[0], height):
            found.append((ref, slice(first, first + own)))
    return found


def key_order(count):
    order = [0]
    bit = count // 2
    while bit:
        order += [o ^ bit for o in order]
        bit //= 2
    return order


def fill_bias(bias, ids, first_key, first_query, member, causal):
    keys_count, own = bias.shape
    count = keys_count // own
    lines = ids[:, :own]
    numbers = lax.broadcasted_iota(jnp.int32, lines.shape, 0)

    def pick(row):
        return jnp.sum(jnp.where(numbers == row, lines, 0.0), axis=0, keepdims=True)

    queries = pick(first_query + member)
    for number, offset in enumerate(key_order(count)):
        peer = jnp.bitwise_xor(member, offset)
        line = jnp.broadcast_to(pick(first_key + peer), (128, own)).T
        line = jnp.concatenate([line] * (own // 128), axis=1)
        term = mask_bias(line, queries)
        if causal:
            keys = lax.broadcasted_iota(jnp.int32, term.shape, 0) + (peer - member) * own
            term = jnp.where(keys <= lax.broadcasted_iota(jnp.int32, term.shape, 1), term, NEGATIVE)
        bias[number * own : (number + 1) * own, :] = term


def attend(q, kv, bias, mixed, stats):
    features = q.shape[1]

    def one_pair(pair, carry):
        columns = pair_columns(pair)
        o, logsum = pair_forward(
            q[:, columns], kv[:, columns], kv[:, pair_columns(pair, features)], bias[...]
        )
        mixed[:, columns] = o
        stats[pair] = logsum
        return carry

    lax.fori_loop(0, features // PAIR, one_pair, 0)


def project(blocks, weight, columns, target):
    for number, (ref, rows) in enumerate(blocks):
        own = rows.stop - rows.start
        target[number * own : (number + 1) * own, :] = nn(ref[rows, :], weight[:, columns]).astype(BF)


def encoder_forward(place, many, refs):
    pieces = refs[:many]
    (w_in, w_out, w_up, w_down, gains, biases,
     q, kv, stats, mixed, normed_a, inverse_a, normed_b, inverse_b, memory, bias, ids) = refs[many:]
    own, features = q.shape
    blocks = blocks_of(pieces, pieces[0].shape[0], own)
    ids[...] = pieces[0][own:, :].astype(F32)
    q[...] = nn(pieces[0][:own, :], w_in[:, :features]).astype(BF)
    project(blocks, w_in, slice(features, 3 * features), kv)
    fill_bias(bias, ids, 0, 0, place[0], False)
    attend(q, kv, bias, mixed, stats)
    v = pieces[0][:own, :].astype(F32) + nn(mixed[...].astype(BF), w_out[...])
    normed, inverse = norm(v)
    normed_a[...] = normed
    inverse_a[...] = inverse
    x1 = normed * gains[0:1, :] + biases[0:1, :]
    pre = nn(x1.astype(BF), w_up[...])
    hidden = (pre * sigmoid(pre)).astype(BF)
    normed, inverse = norm(x1 + nn(hidden, w_down[...]))
    normed_b[...] = normed
    inverse_b[...] = inverse
    memory[...] = (normed * gains[1:2, :] + biases[1:2, :]).astype(BF)


def decoder_self_forward(place, many, refs):
    pieces = refs[:many]
    payload, w_in, w_out, q, kv, stats, mixed, normed_c, inverse_c, bias, ids = refs[many:]
    own, features = q.shape
    count = kv.shape[0] // own
    ids[...] = payload[own:, :].astype(F32)
    q[...] = nn(pieces[0][...], w_in[:, :features]).astype(BF)
    project(blocks_of(pieces, own, own), w_in, slice(features, 3 * features), kv)
    fill_bias(bias, ids, count, count, place[0], True)
    attend(q, kv, bias, mixed, stats)
    v = pieces[0][...].astype(F32) + nn(mixed[...].astype(BF), w_out[...])
    normed, inverse = norm(v)
    normed_c[...] = normed
    inverse_c[...] = inverse


def decoder_middle(place, many, refs):
    pieces = refs[:many]
    (payload, normed_c, out_grad, w_q, w_kv, w_out, w_up, w_down, gains, biases,
     send, keep, dec_out, q, kv, stats, mixed, y1_low, normed_d, inverse_d, d_second, vectors,
     bias, ids, product) = refs[many:]
    own = q.shape[0]
    count = kv.shape[0] // own
    ids[...] = payload[own:, :].astype(F32)
    y1 = normed_c[...] * gains[0:1, :] + biases[0:1, :]
    y1_low[...] = y1.astype(BF)
    q[...] = nn(y1_low[...], w_q[...]).astype(BF)
    project(blocks_of(pieces, own, own), w_kv, slice(None), kv)
    fill_bias(bias, ids, 0, count, place[0], False)
    attend(q, kv, bias, mixed, stats)
    normed, inverse = norm(y1 + nn(mixed[...].astype(BF), w_out[...]))
    normed_d[...] = normed
    inverse_d[...] = inverse
    y2 = normed * gains[1:2, :] + biases[1:2, :]
    y2_low = y2.astype(BF)
    pre = nn(y2_low, w_up[...])
    act, slope = silu_parts(pre)
    hidden = act.astype(BF)
    normed, inverse = norm(y2 + nn(hidden, w_down[...]))
    dec_out[...] = (normed * gains[2:3, :] + biases[2:3, :]).astype(BF)
    dv, gain_grad, bias_grad = norm_back(
        out_grad[...].astype(F32), normed, inverse, gains[2:3, :]
    )
    vectors[0:1, :] = gain_grad
    vectors[1:2, :] = bias_grad
    dv_low = dv.astype(BF)
    d_pre = (nt(dv_low, w_down[...]) * slope).astype(BF)
    d_second[...] = dv + nt(d_pre, w_up[...])
    offset = emit(place[1], product, y2_low, d_pre, send, keep, 0)
    emit(place[1], product, hidden, dv_low, send, keep, offset)


def cross_back(place, many, refs):
    (d_second, payload, q, kv, stats, mixed, normed_d, inverse_d, normed_c, inverse_c,
     w_q, w_kv, w_out, gains,
     memory_keep, memory_send, dq, dkv, dv_low, d_target, vectors, bias, ids, grad) = refs
    own = q.shape[0]
    count = kv.shape[0] // own
    half = memory_keep.shape[0]
    ids[...] = payload[own:, :].astype(F32)
    fill_bias(bias, ids, 0, count, place[0], False)
    dv, gain_grad, bias_grad = norm_back(
        d_second[...], normed_d[...], inverse_d[...], gains[1:2, :]
    )
    vectors[0:1, :] = gain_grad
    vectors[1:2, :] = bias_grad
    dv_low[...] = dv.astype(BF)
    grad[...] = nt(dv_low[...], w_out[...]).astype(BF)
    cross_backward(q, kv, mixed, grad, bias, stats, dq, dkv)
    memory_send[...] = nt(dkv[half:, :], w_kv[...]).astype(BF)
    memory_keep[...] = nt(dkv[:half, :], w_kv[...]).astype(BF)
    d_first = dv + nt(dq[...], w_q[...])
    dv, gain_grad, bias_grad = norm_back(d_first, normed_c[...], inverse_c[...], gains[0:1, :])
    vectors[2:3, :] = gain_grad
    vectors[3:4, :] = bias_grad
    d_target[...] = dv


def whole(blocks, target):
    for number, (ref, rows) in enumerate(blocks):
        own = rows.stop - rows.start
        target[number * own : (number + 1) * own, :] = ref[rows, :]
    return target[...]


def cross_weights(place, many, refs):
    memory = refs[:many]
    y1_low, dq, dkv, mixed, dv_low, send, keep, product, tokens = refs[many:]
    own = y1_low.shape[0]
    offset = emit(place[1], product, y1_low[...], dq[...], send, keep, 0)
    offset = emit(
        place[1], product, whole(blocks_of(memory, own, own), tokens), dkv[...], send, keep, offset
    )
    emit(place[1], product, mixed[...].astype(BF), dv_low[...], send, keep, offset)


def decoder_self_back(place, many, refs):
    pieces = refs[:many]
    (d_target, payload, q, kv, stats, mixed, w_in, w_out, send_c, keep_c,
     target_keep, target_send, send, keep,
     bias, ids, product, grad, dq, dkv, tokens) = refs[many:]
    own, features = q.shape
    count = kv.shape[0] // own
    half = target_keep.shape[0]
    ids[...] = payload[own:, :].astype(F32)
    fill_bias(bias, ids, count, count, place[0], True)
    dv = d_target[...]
    dv_low = dv.astype(BF)
    grad[...] = nt(dv_low, w_out[...]).astype(BF)
    cross_backward(q, kv, mixed, grad, bias, stats, dq, dkv)
    target_send[...] = nt(dkv[half:, :], w_in[:, features:]).astype(BF)
    term = nt(dkv[:half, :], w_in[:, features:])
    target_keep[own:, :] = term[own:].astype(BF)
    target_keep[:own, :] = (term[:own] + dv + nt(dq[...], w_in[:, :features])).astype(BF)
    offset = send_c.shape[1]
    send[:, :offset, :] = send_c[...]
    keep[:, :offset, :] = keep_c[...]
    offset = emit(place[1], product, pieces[0][...], dq[...], send, keep, offset)
    offset = emit(
        place[1], product, whole(blocks_of(pieces, own, own), tokens), dkv[...], send, keep, offset
    )
    emit(place[1], product, mixed[...].astype(BF), dv_low, send, keep, offset)


def encoder_ffn_back(place, many, refs):
    d_memory = refs[:many]
    (normed_a, inverse_a, normed_b, inverse_b, w_up, w_down, gains, biases,
     send, keep, d_source, vectors, product) = refs[many:]
    own = normed_a.shape[0]
    du = d_memory[0][:own, :].astype(F32)
    for piece in d_memory[1:]:
        du = du + piece[:own, :].astype(F32)
    dv, gain_grad, bias_grad = norm_back(du, normed_b[...], inverse_b[...], gains[1:2, :])
    vectors[0:1, :] = gain_grad
    vectors[1:2, :] = bias_grad
    dv_low = dv.astype(BF)
    x1_low = (normed_a[...] * gains[0:1, :] + biases[0:1, :]).astype(BF)
    act, slope = silu_parts(nn(x1_low, w_up[...]))
    hidden = act.astype(BF)
    d_pre = (nt(dv_low, w_down[...]) * slope).astype(BF)
    d_mid = dv + nt(d_pre, w_up[...])
    dv, gain_grad, bias_grad = norm_back(d_mid, normed_a[...], inverse_a[...], gains[0:1, :])
    vectors[2:3, :] = gain_grad
    vectors[3:4, :] = bias_grad
    d_source[...] = dv
    offset = emit(place[1], product, x1_low, d_pre, send, keep, 0)
    emit(place[1], product, hidden, dv_low, send, keep, offset)


def encoder_attention_back(place, many, refs):
    (payload, d_source, q, kv, stats, mixed, w_in, w_out,
     source_keep, source_send, dq, dkv, dv_low, bias, ids, grad) = refs
    own, features = q.shape
    half = source_keep.shape[0]
    ids[...] = payload[own:, :].astype(F32)
    fill_bias(bias, ids, 0, 0, place[0], False)
    dv = d_source[...]
    dv_low[...] = dv.astype(BF)
    grad[...] = nt(dv_low[...], w_out[...]).astype(BF)
    cross_backward(q, kv, mixed, grad, bias, stats, dq, dkv)
    source_send[...] = nt(dkv[half:, :], w_in[:, features:]).astype(BF)
    term = nt(dkv[:half, :], w_in[:, features:])
    source_keep[own:, :] = term[own:].astype(BF)
    source_keep[:own, :] = (term[:own] + dv + nt(dq[...], w_in[:, :features])).astype(BF)


def encoder_attention_weights(place, many, refs):
    pieces = refs[:many]
    (dq, dkv, mixed, dv_low, vectors_e, vectors_cd, vectors_ab,
     send, keep, product, tokens) = refs[many:]
    own, features = dq.shape
    blocks = blocks_of(pieces, pieces[0].shape[0], own)
    offset = emit(place[1], product, pieces[0][:own, :], dq[...], send, keep, 0)
    offset = emit(place[1], product, whole(blocks, tokens), dkv[...], send, keep, offset)
    offset = emit(place[1], product, mixed[...].astype(BF), dv_low[...], send, keep, offset)
    rows = jnp.concatenate(
        [vectors_e[...], vectors_cd[...], vectors_ab[...],
         jnp.zeros((VECTOR_ROWS - 10, features), F32)], axis=0,
    ).astype(BF)
    for slot in range(send.shape[0]):
        send[slot, offset : offset + VECTOR_ROWS, :] = rows
        keep[slot, offset : offset + VECTOR_ROWS, :] = rows


def call(kernel, place, many, operands, outs, scratch, weight, ties=()):
    in_specs = [pl.BlockSpec(memory_space=pltpu.SMEM)]
    in_specs += [pl.BlockSpec(memory_space=pltpu.VMEM)] * len(operands)
    in_specs += [pl.BlockSpec(memory_space=pl.ANY)] * len(ties)
    count = len(operands)
    outs = [jax.ShapeDtypeStruct(shape, dtype) for shape, dtype in outs]
    moved = sum(a.size * a.dtype.itemsize for a in (*operands, *outs))
    return pl.pallas_call(
        lambda place, *refs: kernel(place, many, refs[:count] + refs[count + len(ties) :]),
        name=kernel.__name__,
        out_shape=outs,
        in_specs=in_specs,
        out_specs=[pl.BlockSpec(memory_space=pltpu.VMEM)] * len(outs),
        scratch_shapes=[pltpu.VMEM(shape, dtype) for shape, dtype in scratch],
        compiler_params=pltpu.CompilerParams(vmem_limit_bytes=28 * 1024 * 1024),
        cost_estimate=pl.CostEstimate(
            flops=int(weight * 1.15e9), bytes_accessed=int(moved), transcendentals=0
        ),
    )(place, *operands, *ties)


def exchange(part, bit, devices):
    return lax.ppermute(part, "dp", [(i, i ^ bit) for i in range(devices)])


def gather_group(own, count, devices):
    arrays, held, bit = [own], own, count // 2
    while bit:
        arrays.append(exchange(held, bit, devices))
        if bit > 1:
            held = jnp.concatenate([held, arrays[-1]], axis=0)
        bit //= 2
    return arrays


def scatter_group(keep, send, count, devices):
    arrays, bit = [keep], 1
    while bit < count:
        received = exchange(send, bit, devices)
        arrays.append(received)
        half = received.shape[0] // 2
        if 2 * bit < count:
            send = keep[half:] + received[half:]
            keep = keep[:half] + received[:half]
        bit *= 2
    return arrays


def first_sum(arrays, own):
    total = arrays[0][:own].astype(F32)
    for a in arrays[1:]:
        total = total + a[:own].astype(F32)
    return total


def add_parts(place, many, refs):
    kept_a, came_a, kept_b, came_b, send_a, keep_a, send_b, keep_b = refs
    cut, half = keep_a.shape[1], keep_a.shape[0]
    first = kept_b.shape[1] - keep_b.shape[1]

    def total(kept, came, index, rows):
        return (kept[index, rows, :].astype(F32) + came[index, rows, :].astype(F32)).astype(BF)

    for number in range(half):
        send_a[number] = total(kept_a, came_a, 2 * number + 1, slice(0, cut))
        keep_a[number] = total(kept_a, came_a, 2 * number, slice(0, cut))
        send_b[number] = total(kept_b, came_b, half + number, slice(first, None))
        keep_b[number] = total(kept_b, came_b, number, slice(first, None))


def add_last(place, many, refs):
    kept_a, came_a, kept_b, came_b, total = refs
    cut = kept_a.shape[1]
    total[:cut, :] = (kept_a[0].astype(F32) + came_a[0].astype(F32)).astype(BF)
    total[cut:, :] = (kept_b[0].astype(F32) + came_b[0].astype(F32)).astype(BF)


class DpSum:
    def __init__(self, place, send, keep, devices):
        self.place, self.devices, self.bits = place, devices, devices.bit_length() - 2
        self.rows, self.cut = keep.shape[1], keep.shape[1] // 32 * 16
        self.kept, self.sent, self.stage = (keep, keep), send, 0

    def step(self):
        devices, bits = self.devices, self.bits
        if self.stage == 0:
            came = exchange(self.sent, 1, devices)
            self.came = (came, came)
        else:
            ways = (1 << self.stage, 1 << (bits + 1 - self.stage))
            self.came = tuple(exchange(a, way, devices) for a, way in zip(self.sent, ways))
        arrived = list({id(a): a for a in self.came}.values())
        operands = [self.kept[0], self.came[0], self.kept[1], self.came[1]]
        features = operands[0].shape[2]
        if self.stage < bits:
            half = operands[0].shape[0] // 2
            one = ((half, self.cut, features), BF)
            other = ((half, self.rows - self.cut, features), BF)
            send_a, keep_a, send_b, keep_b = call(
                add_parts, self.place, 0, operands, [one, one, other, other], [], 2
            )
            self.sent, self.kept = (send_a, send_b), (keep_a, keep_b)
        else:
            self.total = call(
                add_last, self.place, 0, operands, [((self.rows, features), BF)], [], 1
            )[0]
        self.stage += 1
        return arrived

    def finish(self):
        while self.stage <= self.bits:
            self.step()
        return self.total


def sum_over_src(own, count):
    total = own
    carried = own
    for hop in range(1, count):
        pairs = [(hop - 1, hop), (count - hop, count - hop - 1)]
        if count % 2 and hop == count - hop - 1:
            received = lax.ppermute(carried, "src", pairs[:1]) + lax.ppermute(
                carried, "src", pairs[1:]
            )
        else:
            received = lax.ppermute(carried, "src", pairs)
        total = total + received
        carried = own + received
    return total


def local(
    src_tok, src_ids, tgt_tok, tgt_ids, out_grad,
    enc_attn_in, enc_attn_out, enc_ffn_in, enc_ffn_out, enc_gains, enc_biases,
    dec_self_in, dec_self_out, dec_cross_q, dec_cross_kv, dec_cross_out,
    dec_ffn_in, dec_ffn_out, dec_gains, dec_biases,
):
    count, devices = lax.axis_size("src"), lax.axis_size("dp")
    _, own, features = src_tok.shape
    length = tgt_tok.shape[1]
    pairs = features // PAIR
    hidden = enc_ffn_in.shape[1]
    me, me_dp = lax.axis_index("src"), lax.axis_index("dp")
    place = jnp.stack([lax.rem(me_dp, count), me_dp]).astype(jnp.int32)
    turn = count // 2
    inward = []
    for row in range(devices):
        column, core = divmod(row, 2)
        there = column % turn if core == 0 else count - 1 - column % turn
        for part in range(count):
            member = column // turn * count + part
            inward.append((row * count + part, member * count + there))
    outward = [(there, here) for here, there in inward]

    def enter(a):
        return lax.ppermute(a, ("dp", "src"), inward)

    def leave(a):
        return lax.ppermute(a, ("dp", "src"), outward)

    first = me * own
    ids = jnp.concatenate([src_ids.reshape(count, own), tgt_ids.reshape(count, own)], axis=0)
    ids = jnp.pad(ids, ((0, ID_ROWS - 2 * count), (0, features - own))).astype(BF)
    payload = enter(jnp.concatenate([src_tok[0], ids], axis=0))
    source_pieces = gather_group(payload, count, devices)
    target = enter(lax.dynamic_slice_in_dim(tgt_tok[0], first, own, 0))
    own_grad = enter(lax.dynamic_slice_in_dim(out_grad[0], first, own, 0))
    target_pieces = gather_group(target, count, devices)
    many = len(source_pieces)

    narrow, half = (own, features), (length // 2, features)
    shard = features // devices
    column = ((own, 1), F32)
    pair_stats = ((pairs, 2, own), F32)
    all_keys = ((length, 2 * features), BF)
    id_scratch = ((ID_ROWS, features), F32)
    bias_scratch = ((length, own), F32)
    small_product = ((devices, shard, features), BF)
    product = ((devices, hidden // devices, features), BF)

    def bucket(rows):
        return [((devices // 2, rows, features), BF)] * 2

    ffn_rows = 2 * shard * (hidden // features)

    q_e, kv_e, stats_e, mixed_e, normed_a, inverse_a, normed_b, inverse_b, memory = call(
        encoder_forward, place, many,
        [*source_pieces, enc_attn_in, enc_attn_out, enc_ffn_in, enc_ffn_out, enc_gains, enc_biases],
        [(narrow, BF), all_keys, pair_stats, (narrow, F32), (narrow, F32), column, (narrow, F32),
         column, (narrow, BF)],
        [bias_scratch, id_scratch],
        12,
    )
    memory_pieces = gather_group(memory, count, devices)
    q_d, kv_d, stats_d, mixed_d, normed_c, inverse_c = call(
        decoder_self_forward, place, many,
        [*target_pieces, payload, dec_self_in, dec_self_out],
        [(narrow, BF), all_keys, pair_stats, (narrow, F32), (narrow, F32), column],
        [bias_scratch, id_scratch],
        10,
    )
    (send_f, keep_f, out_own, q_c, kv_c, stats_c, mixed_c, y1_low, normed_d, inverse_d, d_second,
     vectors_e) = call(
        decoder_middle, place, many,
        [*memory_pieces, payload, normed_c, own_grad, dec_cross_q, dec_cross_kv, dec_cross_out,
         dec_ffn_in, dec_ffn_out, dec_gains, dec_biases],
        [*bucket(ffn_rows), (narrow, BF), (narrow, BF), all_keys, pair_stats, (narrow, F32),
         (narrow, BF), (narrow, F32), column, (narrow, F32), ((2, features), F32)],
        [bias_scratch, id_scratch, product],
        18,
    )
    sum_f = DpSum(place, send_f, keep_f, devices)
    core_f = sum_f.step()
    out_back = leave(out_own)
    dec_out = lax.all_gather(out_back, "src", axis=0, tiled=True)
    memory_keep, memory_send, dq_c, dkv_c, dv_d, d_target, vectors_cd = call(
        cross_back, place, many,
        [d_second, payload, q_c, kv_c, stats_c, mixed_c, normed_d, inverse_d, normed_c, inverse_c,
         dec_cross_q, dec_cross_kv, dec_cross_out, dec_gains],
        [(half, BF), (half, BF), (narrow, BF), all_keys, (narrow, BF), (narrow, F32),
         ((4, features), F32)],
        [bias_scratch, id_scratch, (narrow, BF)],
        15,
    )
    memory_grads = scatter_group(memory_keep, memory_send, count, devices)
    send_c, keep_c = call(
        cross_weights, place, many,
        [*memory_pieces, y1_low, dq_c, dkv_c, mixed_c, dv_d],
        bucket(4 * shard),
        [small_product, ((length, features), BF)],
        5, [*core_f, out_back],
    )
    first_f = sum_f.step()
    target_keep, target_send, send_d, keep_d = call(
        decoder_self_back, place, many,
        [*target_pieces, d_target, payload, q_d, kv_d, stats_d, mixed_d, dec_self_in, dec_self_out,
         send_c, keep_c],
        [(half, BF), (half, BF), *bucket(8 * shard)],
        [bias_scratch, id_scratch, small_product, (narrow, BF), (narrow, BF), all_keys,
         ((length, features), BF)],
        15, [*memory_grads[1:2]],
    )
    sum_d = DpSum(place, send_d, keep_d, devices)
    core_d = sum_d.step()
    target_grads = scatter_group(target_keep, target_send, count, devices)
    send_u, keep_u, d_source, vectors_ab = call(
        encoder_ffn_back, place, len(memory_grads),
        [*memory_grads, normed_a, inverse_a, normed_b, inverse_b, enc_ffn_in, enc_ffn_out,
         enc_gains, enc_biases],
        [*bucket(ffn_rows), (narrow, F32), ((4, features), F32)],
        [product],
        8, first_f,
    )
    second_f = sum_f.step()
    sum_u = DpSum(place, send_u, keep_u, devices)
    core_u = sum_u.step()
    source_keep, source_send, dq_e, dkv_e, dv_a = call(
        encoder_attention_back, place, many,
        [payload, d_source, q_e, kv_e, stats_e, mixed_e, enc_attn_in, enc_attn_out],
        [(half, BF), (half, BF), (narrow, BF), all_keys, (narrow, BF)],
        [bias_scratch, id_scratch, (narrow, BF)],
        13, [*second_f, *core_d, target_grads[1]],
    )
    source_grads = scatter_group(source_keep, source_send, count, devices)
    send_a, keep_a = call(
        encoder_attention_weights, place, many,
        [*source_pieces, dq_e, dkv_e, mixed_e, dv_a, vectors_e, vectors_cd, vectors_ab],
        bucket(4 * shard + VECTOR_ROWS),
        [small_product, ((length, features), BF)],
        5, [*core_u, *target_grads[2:]],
    )
    sum_a = DpSum(place, send_a, keep_a, devices)
    tgt_grad = lax.all_gather(
        leave(first_sum(target_grads, own).astype(BF)), "src", axis=0, tiled=True
    ).astype(F32)
    src_grad = leave(first_sum(source_grads, own).astype(BF)).astype(F32)
    ffn_d, attn_d, ffn_e, attn_e = (
        sum_over_src(one.finish(), count).astype(F32) for one in (sum_f, sum_d, sum_u, sum_a)
    )

    def wide(rows):
        return jnp.concatenate(jnp.split(rows, rows.shape[0] // shard, axis=0), axis=1)

    up = shard * (hidden // features)
    vectors = attn_e[4 * shard :]
    vectors = lax.dynamic_slice_in_dim(vectors, me_dp * shard, shard, 1)
    return (
        dec_out[None],
        src_grad[None],
        tgt_grad[None],
        wide(attn_e[: 3 * shard]),
        attn_e[3 * shard : 4 * shard],
        wide(ffn_e[:up]),
        ffn_e[up:],
        jnp.stack([vectors[8], vectors[6]]),
        jnp.stack([vectors[9], vectors[7]]),
        wide(attn_d[4 * shard : 7 * shard]),
        attn_d[7 * shard :],
        attn_d[:shard],
        wide(attn_d[shard : 3 * shard]),
        attn_d[3 * shard : 4 * shard],
        wide(ffn_d[:up]),
        ffn_d[up:],
        jnp.stack([vectors[4], vectors[2], vectors[0]]),
        jnp.stack([vectors[5], vectors[3], vectors[1]]),
    )


def solution(mesh):
    row, part = P("dp", None, None), P("dp", "src", None)
    line, rows, columns = P("dp", None), P("dp", None), P(None, "dp")
    in_specs = (part, line, row, line, row) + (P(),) * 15
    out_specs = (
        row, part, row, rows, rows, rows, rows, columns, columns,
        rows, rows, rows, rows, rows, rows, rows, columns, columns,
    )
    return jax.shard_map(local, mesh=mesh, in_specs=in_specs, out_specs=out_specs, check_vma=False)
```

```python
import functools
import math

import jax
import jax.numpy as jnp
from jax import lax
from jax.experimental import pallas as pl
from jax.experimental.pallas import tpu as pltpu
from jax.sharding import PartitionSpec as P

HEAD_DIM = 64
PAIR = 2 * HEAD_DIM
EPS = 1e-05
NEGATIVE = -1e30
BF = jnp.bfloat16
F32 = jnp.float32
BLOCK = 1024
VECTOR_ROWS = 32
ID_ROWS = 16
LIMIT = 40


def dot(former, latter, dims):
    return lax.dot_general(former, latter, (dims, ((), ())), preferred_element_type=F32)


def nn(former, latter):
    return dot(former, latter, ((1,), (0,)))


def nt(former, latter):
    return dot(former, latter, ((1,), (1,)))


def tn(former, latter):
    return dot(former, latter, ((0,), (0,)))


def norm(v):
    centred = v - jnp.mean(v, axis=-1, keepdims=True)
    inverse = lax.rsqrt(jnp.mean(centred * centred, axis=-1, keepdims=True) + EPS)
    return centred * inverse, inverse


def norm_back(du, normed, inverse, gain):
    gain_grad = jnp.sum(du * normed, axis=0, keepdims=True)
    bias_grad = jnp.sum(du, axis=0, keepdims=True)
    scaled = du * gain
    mean = jnp.mean(scaled, axis=-1, keepdims=True)
    slope = jnp.mean(scaled * normed, axis=-1, keepdims=True)
    return inverse * (scaled - mean - normed * slope), gain_grad, bias_grad


def head_halves(pair, scale):
    wide = pair.astype(F32) * scale
    first = lax.broadcasted_iota(jnp.int32, wide.shape, 1) < HEAD_DIM
    return [jnp.where(first, wide, 0.0).astype(BF), jnp.where(first, 0.0, wide).astype(BF)]


def pair_columns(pair, offset=0):
    return pl.ds(pl.multiple_of(pair * PAIR + offset, PAIR), PAIR)


def mask_bias(key_ids, query_ids):
    return jnp.where(key_ids == query_ids, 0.0, NEGATIVE)


def pair_forward(q, k, v, bias):
    queries = head_halves(q, HEAD_DIM**-0.5)
    values = v.T
    mixed, stats = [], []
    for head in range(2):
        s = nt(k, queries[head]) + bias
        maximum = jnp.max(s, axis=0, keepdims=True)
        e = jnp.exp(s - maximum)
        total = jnp.sum(e, axis=0, keepdims=True)
        o = nn(values[head * HEAD_DIM : (head + 1) * HEAD_DIM], e.astype(BF))
        mixed.append(o * (1.0 / total))
        stats.append(maximum + jnp.log(total))
    return jnp.concatenate(mixed, axis=0).T, jnp.concatenate(stats, axis=0)


def pair_delta(o, grad):
    product = (o * grad.astype(F32)).T
    return (
        jnp.sum(product[:HEAD_DIM], axis=0, keepdims=True),
        jnp.sum(product[HEAD_DIM:], axis=0, keepdims=True),
    )


def block_backward(qs, gs, k, v, keys, bias, stats, deltas):
    dq, dk, dv = [], None, None
    for head in range(2):
        s = nt(k, qs[head]) + bias
        p = jnp.exp(s - stats[head : head + 1])
        ds = (p * (nt(v, gs[head]) - deltas[head])).astype(BF)
        p = p.astype(BF)
        dq.append(nn(keys[head * HEAD_DIM : (head + 1) * HEAD_DIM], ds))
        dk_term, dv_term = nn(ds, qs[head]), nn(p, gs[head])
        dk = dk_term if dk is None else dk + dk_term
        dv = dv_term if dv is None else dv + dv_term
    return jnp.concatenate(dq, axis=0), dk, dv


def cross_backward(q_ref, kv_ref, o_ref, g_ref, bias_ref, stats_ref, dq_ref, dkv_ref):
    features = q_ref.shape[1]
    keys_count = kv_ref.shape[0]

    def one_pair(pair, carry):
        columns = pair_columns(pair)
        value_columns = pair_columns(pair, features)
        q, g = q_ref[:, columns], g_ref[:, columns]
        qs = head_halves(q, HEAD_DIM**-0.5)
        gs = head_halves(g, 1.0)
        deltas = pair_delta(o_ref[:, columns], g)
        stats = stats_ref[pair]
        total = None
        for first in range(0, keys_count, BLOCK):
            rows = slice(first, first + BLOCK)
            k = kv_ref[rows, columns]
            term, dk, dv = block_backward(
                qs, gs, k, kv_ref[rows, value_columns], k.T, bias_ref[rows, :], stats, deltas
            )
            dkv_ref[rows, columns] = dk.astype(BF)
            dkv_ref[rows, value_columns] = dv.astype(BF)
            total = term if total is None else total + term
        dq_ref[:, columns] = (total.T * HEAD_DIM**-0.5).astype(BF)
        return carry

    lax.fori_loop(0, features // PAIR, one_pair, 0)


def emit(me_dp, product, former, latter, send, keep, offset):
    devices = 2 * send.shape[0]
    width = product.shape[2]
    height = former.shape[1]
    rows = height // devices
    for first in range(0, latter.shape[1], width):
        term = tn(former, latter[:, first : first + width]).astype(BF)
        product[:, :rows, :] = term.reshape(devices, rows, width)
        for slot in range(devices):
            target = send if slot % 2 else keep
            target[slot // 2, offset : offset + rows, :] = product[
                jnp.bitwise_xor(me_dp, slot), :rows, :
            ]
        offset += rows
    return offset


def sigmoid(v):
    return 1.0 / (1.0 + jnp.exp(-v))


def silu_parts(pre):
    squashed = sigmoid(pre)
    return pre * squashed, squashed * (1.0 + pre * (1.0 - squashed))


def near_order(count):
    order, bit = [0], 1
    while bit < count:
        order += [o ^ bit for o in order]
        bit *= 2
    return order


def near_blocks(refs, own, count):
    found = blocks_of(refs, own, own)
    return [found[near_order(count).index(o)] for o in key_order(count)]


def blocks_of(refs, height, own):
    found = []
    for ref in refs:
        for first in range(0, ref.shape[0], height):
            found.append((ref, slice(first, first + own)))
    return found


def key_order(count):
    order = [0]
    bit = count // 2
    while bit:
        order += [o ^ bit for o in order]
        bit //= 2
    return order


def spread_order(count):
    order, bit = [0], count // 2
    while bit:
        order += [o ^ bit for o in order]
        bit //= 2
    return order


def fill_bias(bias, ids, first_key, first_query, member, causal):
    keys_count, own = bias.shape
    count = keys_count // own
    lines = ids[:, :own]
    numbers = lax.broadcasted_iota(jnp.int32, lines.shape, 0)

    def pick(row):
        return jnp.sum(jnp.where(numbers == row, lines, 0.0), axis=0, keepdims=True)

    queries = pick(first_query + member)
    for number, offset in enumerate(key_order(count)):
        peer = jnp.bitwise_xor(member, offset)
        line = jnp.broadcast_to(pick(first_key + peer), (128, own)).T
        line = jnp.concatenate([line] * (own // 128), axis=1)
        term = mask_bias(line, queries)
        if causal:
            keys = lax.broadcasted_iota(jnp.int32, term.shape, 0) + (peer - member) * own
            term = jnp.where(keys <= lax.broadcasted_iota(jnp.int32, term.shape, 1), term, NEGATIVE)
        bias[number * own : (number + 1) * own, :] = term


def attend(q, kv, bias, mixed, stats):
    features = q.shape[1]

    def one_pair(pair, carry):
        columns = pair_columns(pair)
        o, logsum = pair_forward(
            q[:, columns], kv[:, columns], kv[:, pair_columns(pair, features)], bias[...]
        )
        mixed[:, columns] = o
        stats[pair] = logsum
        return carry

    lax.fori_loop(0, features // PAIR, one_pair, 0)


def project(blocks, weight, columns, target):
    for number, (ref, rows) in enumerate(blocks):
        own = rows.stop - rows.start
        target[number * own : (number + 1) * own, :] = nn(ref[rows, :], weight[:, columns]).astype(BF)


def put_norm(target, number, normed, inverse):
    features = normed.shape[1]
    count = target.shape[1] // (features + PAIR)
    target[:, number * features : (number + 1) * features] = normed
    first = count * features + number * PAIR
    target[:, first : first + PAIR] = jnp.broadcast_to(inverse, (inverse.shape[0], PAIR))


def get_norm(source, number, features):
    count = source.shape[1] // (features + PAIR)
    first = count * features + number * PAIR
    return source[:, number * features : (number + 1) * features], source[:, first : first + 1]


def encoder_forward(io, many, refs):
    pieces = refs[:many]
    (names, w_in, w_out, w_up, w_down, gains, biases,
     q, kv, stats, mixed, norms, memory, bias, ids) = refs[many:]
    own, features = q.shape
    blocks = blocks_of(pieces, own, own)
    io.ready(pieces[0], w_in)
    q[...] = nn(pieces[0][...], w_in[:, :features]).astype(BF)
    io.ready(*pieces)
    project(blocks, w_in, slice(features, 3 * features), kv)
    ids[...] = names[...].astype(F32)
    fill_bias(bias, ids, 0, 0, io.place[0], False)
    attend(q, kv, bias, mixed, stats)
    io.flush(q, kv, stats, mixed)
    io.ready(w_out, gains, biases, w_up, w_down)
    v = pieces[0][...].astype(F32) + nn(mixed[...].astype(BF), w_out[...])
    normed, inverse = norm(v)
    put_norm(norms, 0, normed, inverse)
    x1 = normed * gains[0:1, :] + biases[0:1, :]
    pre = nn(x1.astype(BF), w_up[...])
    hidden = (pre * sigmoid(pre)).astype(BF)
    normed, inverse = norm(x1 + nn(hidden, w_down[...]))
    put_norm(norms, 1, normed, inverse)
    memory[...] = (normed * gains[1:2, :] + biases[1:2, :]).astype(BF)


def decoder_self_forward(io, many, refs):
    tokens, names, w_in, w_out, q, kv, stats, mixed, norms, bias, ids = refs
    own, features = q.shape
    count = tokens.shape[0]
    member = io.place[0]
    io.ready(names, tokens, w_in)
    ids[...] = names[...].astype(F32)
    mine = tokens[member]
    q[...] = nn(mine, w_in[:, :features]).astype(BF)
    for number, offset in enumerate(key_order(count)):
        kv[number * own : (number + 1) * own, :] = nn(
            tokens[jnp.bitwise_xor(member, offset)], w_in[:, features:]
        ).astype(BF)
    fill_bias(bias, ids, count, count, member, True)
    attend(q, kv, bias, mixed, stats)
    io.flush(q, kv, stats, mixed)
    io.ready(w_out)
    normed, inverse = norm(mine.astype(F32) + nn(mixed[...].astype(BF), w_out[...]))
    put_norm(norms, 0, normed, inverse)


def decoder_middle(io, many, refs):
    pieces = refs[:many]
    (names, norms, out_grad, w_q, w_kv, w_out, w_up, w_down, gains, biases,
     shards, dec_out, memory_keep, memory_send, d_target, vectors,
     bias, ids, q, kv, stats, mixed, dq, grad, dkv, memory) = refs[many:]
    own, features = q.shape
    count = kv.shape[0] // own
    half = memory_keep.shape[0]
    io.ready(names, norms, gains, biases, w_q)
    ids[...] = names[...].astype(F32)
    normed_c, inverse_c = get_norm(norms, 0, features)
    y1 = normed_c * gains[0:1, :] + biases[0:1, :]
    y1_low = y1.astype(BF)
    q[...] = nn(y1_low, w_q[...]).astype(BF)
    io.ready(w_kv, *pieces)
    project(near_blocks(pieces, own, count), w_kv, slice(None), kv)
    fill_bias(bias, ids, 0, count, io.place[0], False)
    attend(q, kv, bias, mixed, stats)
    io.ready(w_out, w_up, w_down, out_grad)
    mixed_low = mixed[...].astype(BF)
    normed_d, inverse_d = norm(y1 + nn(mixed_low, w_out[...]))
    y2 = normed_d * gains[1:2, :] + biases[1:2, :]
    y2_low = y2.astype(BF)
    act, slope = silu_parts(nn(y2_low, w_up[...]))
    hidden = act.astype(BF)
    normed, inverse = norm(y2 + nn(hidden, w_down[...]))
    dec_out[...] = (normed * gains[2:3, :] + biases[2:3, :]).astype(BF)
    dv, gain_grad, bias_grad = norm_back(
        out_grad[...].astype(F32), normed, inverse, gains[2:3, :]
    )
    vectors[0:1, :] = gain_grad
    vectors[1:2, :] = bias_grad
    dv_low = dv.astype(BF)
    d_pre = (nt(dv_low, w_down[...]) * slope).astype(BF)
    devices, _, width = shards.shape
    offset = 0

    def emit_all(former, latter, offset):
        rows = former.shape[1] // devices
        for first in range(0, latter.shape[1], width):
            term = tn(former, latter[:, first : first + width]).astype(BF)
            shards[:, offset : offset + rows, :] = term.reshape(devices, rows, width)
            offset += rows
        return offset

    offset = emit_all(y2_low, d_pre, offset)
    offset = emit_all(hidden, dv_low, offset)
    io.flush(dec_out)
    d_second = dv + nt(d_pre, w_up[...])
    dv, gain_grad, bias_grad = norm_back(d_second, normed_d, inverse_d, gains[1:2, :])
    vectors[2:3, :] = gain_grad
    vectors[3:4, :] = bias_grad
    dv_low = dv.astype(BF)
    offset = emit_all(mixed_low, dv_low, offset)
    grad[...] = nt(dv_low, w_out[...]).astype(BF)
    cross_backward(q, kv, mixed, grad, bias, stats, dq, dkv)
    offset = emit_all(y1_low, dq[...], offset)
    emit_all(whole(near_blocks(pieces, own, count), memory), dkv[...], offset)
    io.flush(shards)
    memory_send[...] = nt(dkv[half:, :], w_kv[...]).astype(BF)
    memory_keep[...] = nt(dkv[:half, :], w_kv[...]).astype(BF)
    io.flush(memory_send, memory_keep)
    d_first = dv + nt(dq[...], w_q[...])
    dv, gain_grad, bias_grad = norm_back(d_first, normed_c, inverse_c, gains[0:1, :])
    vectors[4:5, :] = gain_grad
    vectors[5:6, :] = bias_grad
    d_target[...] = dv


def whole(blocks, target):
    for number, (ref, rows) in enumerate(blocks):
        own = rows.stop - rows.start
        target[number * own : (number + 1) * own, :] = ref[rows, :]
    return target[...]


def self_back(io, refs, first_id, causal):
    (dv, names, q, kv, stats, mixed, w_in, w_out, keep, send, pack, dkv, bias, ids, grad, dq) = refs
    own, features = q.shape
    half = keep.shape[0]
    io.ready(names, dv, mixed, w_out)
    ids[...] = names[...].astype(F32)
    fill_bias(bias, ids, first_id, first_id, io.place[0], causal)
    dv_low = dv[...].astype(BF)
    pack[own : 2 * own, :] = dv_low
    pack[2 * own :, :] = mixed[...].astype(BF)
    grad[...] = nt(dv_low, w_out[...]).astype(BF)
    io.ready(q, kv, stats)
    cross_backward(q, kv, mixed, grad, bias, stats, dq, dkv)
    pack[:own, :] = dq[...]
    io.flush(pack, dkv)
    io.ready(w_in)
    send[...] = nt(dkv[half:, :], w_in[:, features:]).astype(BF)
    io.flush(send)
    term = nt(dkv[:half, :], w_in[:, features:])
    keep[own:, :] = term[own:].astype(BF)
    keep[:own, :] = (term[:own] + dv[...] + nt(dq[...], w_in[:, :features])).astype(BF)


def decoder_self_back(io, many, refs):
    q, kv = refs[2:4]
    self_back(io, refs, kv.shape[0] // q.shape[0], True)


def encoder_attention_back(io, many, refs):
    self_back(io, refs, 0, False)


def emit_self(io, tokens, pack, dkv, send, keep, product, offset):
    own = pack.shape[0] // 3
    offset = emit(io.place[1], product, tokens[:own, :], pack[:own, :], send, keep, offset)
    offset = emit(io.place[1], product, tokens[...], dkv[...], send, keep, offset)
    return emit(
        io.place[1], product, pack[2 * own :, :], pack[own : 2 * own, :], send, keep, offset
    )


def encoder_ffn_back(io, many, refs):
    d_memory = refs[:many]
    norms, w_up, w_down, gains, biases, d_source, vectors, pack, wide = refs[many:]
    own, features = d_source.shape
    units = w_up.shape[1]
    io.ready(*d_memory, norms, gains, biases)
    du = first_rows(d_memory, own)
    dv, gain_grad, bias_grad = norm_back(du, *get_norm(norms, 1, features), gains[1:2, :])
    vectors[0:1, :] = gain_grad
    vectors[1:2, :] = bias_grad
    dv_low = dv.astype(BF)
    normed_a, inverse_a = get_norm(norms, 0, features)
    x1_low = (normed_a * gains[0:1, :] + biases[0:1, :]).astype(BF)
    pack[:own, :] = x1_low
    pack[own:, :] = dv_low
    io.flush(pack)
    io.ready(w_up, w_down)
    act, slope = silu_parts(nn(x1_low, w_up[...]))
    wide[:, :units] = act.astype(BF)
    d_pre = (nt(dv_low, w_down[...]) * slope).astype(BF)
    wide[:, units:] = d_pre
    io.flush(wide)
    d_mid = dv + nt(d_pre, w_up[...])
    dv, gain_grad, bias_grad = norm_back(d_mid, normed_a, inverse_a, gains[0:1, :])
    vectors[2:3, :] = gain_grad
    vectors[3:4, :] = bias_grad
    d_source[...] = dv


def late_weights(io, many, refs):
    pieces = refs[:many]
    (tokens, pack_d, dkv_d, pack, wide, pack_e, dkv_e, vectors_d, vectors_e,
     send, keep, send_f, keep_f, product, ordered) = refs[many:]
    count, own, features = tokens.shape
    units = wide.shape[1] // 2
    io.ready(tokens, pack_d, dkv_d)
    for number, peer in enumerate(key_order(count)):
        rows = slice(number * own, (number + 1) * own)
        ordered[rows, :] = tokens[jnp.bitwise_xor(io.place[0], peer)]
    offset = emit_self(io, ordered, pack_d, dkv_d, send, keep, product, 0)
    io.ready(*pieces, pack_e, dkv_e, vectors_d, vectors_e)
    whole(blocks_of(pieces, own, own), ordered)
    offset = emit_self(io, ordered, pack_e, dkv_e, send, keep, product, offset)
    rows = jnp.concatenate(
        [vectors_d[...], vectors_e[...], jnp.zeros((VECTOR_ROWS - 10, features), F32)], axis=0
    ).astype(BF)
    for slot in range(send.shape[0]):
        send[slot, offset : offset + VECTOR_ROWS, :] = rows
        keep[slot, offset : offset + VECTOR_ROWS, :] = rows
    io.ready(pack, wide)
    offset = emit(io.place[1], product, pack[:own, :], wide[:, units:], send_f, keep_f, 0)
    emit(io.place[1], product, wide[:, :units], pack[own:, :], send_f, keep_f, offset)


class Far:
    def __init__(self, array):
        self.array = array


class Choice:
    def __init__(self, arrays):
        self.arrays = arrays


class ChosenCopy:
    def __init__(self, place, sources, target, semaphore):
        self.which = place[2]
        self.copies = [pltpu.make_async_copy(a, target, semaphore) for a in sources]

    def start(self):
        for number, copy in enumerate(self.copies):
            pl.when(self.which == number)(copy.start)

    def wait(self):
        self.copies[0].wait()


class Io:
    def __init__(self, place, arriving, leaving):
        self.place, self.arriving, self.leaving, self.gone = place, arriving, leaving, []
        for copy in arriving.values():
            copy.start()

    def ready(self, *refs):
        for ref in refs:
            copy = self.arriving.pop(id(ref), None)
            if copy is not None:
                copy.wait()

    def flush(self, *refs):
        for ref in refs:
            copy = self.leaving.pop(id(ref), None)
            if copy is not None:
                copy.start()
                self.gone.append(copy)

    def finish(self):
        for copy in self.arriving.values():
            copy.wait()
        for copy in self.leaving.values():
            copy.start()
        for copy in [*self.gone, *self.leaving.values()]:
            copy.wait()


class Order:
    def __init__(self, place):
        self.place = place

    def run(self, body, name, operands, outs, in_specs, out_specs, scratch, weight, grid=()):
        moved = sum(math.prod(a.shape) * a.dtype.itemsize for a in (*operands, *outs))
        found = pl.pallas_call(
            body,
            name=name,
            grid=grid,
            out_shape=[jax.ShapeDtypeStruct((3,), jnp.int32), *outs],
            in_specs=[pl.BlockSpec(memory_space=pltpu.SMEM), *in_specs],
            out_specs=[pl.BlockSpec(memory_space=pltpu.SMEM), *out_specs],
            scratch_shapes=scratch,
            compiler_params=pltpu.CompilerParams(vmem_limit_bytes=LIMIT * 1024 * 1024),
            cost_estimate=pl.CostEstimate(
                flops=int(weight * 1.15e9), bytes_accessed=int(moved), transcendentals=0
            ),
        )(self.place, *operands)
        self.place = found[0]
        return list(found[1:])

    def call(self, kernel, many, operands, outs, scratch, weight, ties=()):
        far_out = [i for i, out in enumerate(outs) if len(out) == 3]
        groups, flat, spaces, held = [], [], [], []
        for a in operands:
            if isinstance(a, (Far, Choice)):
                arrays = a.arrays if isinstance(a, Choice) else [a.array]
                held.append(arrays[0])
                arrays = [pltpu.with_memory_space_constraint(one, pltpu.HBM) for one in arrays]
                space = pltpu.HBM
            else:
                arrays, space = [a], pltpu.VMEM
            groups.append((slice(len(flat), len(flat) + len(arrays)), space == pltpu.HBM))
            flat += arrays
            spaces += [pl.BlockSpec(memory_space=space)] * len(arrays)
        outs = [jax.ShapeDtypeStruct(*out[:2]) for out in outs]
        count, tied, far_in = len(flat), len(ties), len(held)

        def wrapped(place, *refs):
            sources, refs = refs[:count], refs[count + tied :]
            after, results, refs = refs[0], list(refs[1 : 1 + len(outs)]), refs[1 + len(outs) :]
            here, refs = list(refs[:far_in]), refs[far_in:]
            inputs, arriving, leaving = [], {}, {}
            for places, far in groups:
                if far:
                    target = here[len(arriving)]
                    semaphore = refs[-2].at[len(arriving)]
                    arriving[id(target)] = ChosenCopy(place, sources[places], target, semaphore)
                    if places.stop - places.start == 1:
                        arriving[id(target)] = arriving[id(target)].copies[0]
                    inputs.append(target)
                else:
                    inputs.append(sources[places.start])
            for number, i in enumerate(far_out):
                target = refs[number]
                leaving[id(target)] = pltpu.make_async_copy(target, results[i], refs[-1].at[number])
                results[i] = target
            refs = refs[len(far_out) : -2]
            for i in range(3):
                after[i] = place[i]
            io = Io(place, arriving, leaving)
            kernel(io, many, (*inputs, *results, *refs))
            io.finish()

        held += [outs[i] for i in far_out]
        out_specs = [
            pl.BlockSpec(memory_space=pltpu.HBM if i in far_out else pltpu.VMEM)
            for i in range(len(outs))
        ]
        outs = [pltpu.HBM(a.shape, a.dtype) if i in far_out else a for i, a in enumerate(outs)]
        return self.run(
            wrapped, kernel.__name__, [*flat, *ties], outs,
            spaces + [pl.BlockSpec(memory_space=pl.ANY)] * tied, out_specs,
            [pltpu.VMEM(a.shape, a.dtype) for a in held]
            + [pltpu.VMEM(shape, dtype) for shape, dtype in scratch]
            + [pltpu.SemaphoreType.DMA((max(1, n),)) for n in (far_in, len(far_out))],
            weight,
        )

    def batch(self, tasks, weight, ties=()):
        operands = [a for task in tasks for a in task[1]]
        outs = [out for task in tasks for out in task[2]]

        def batch(io, many, refs):
            inputs, results = list(refs[: len(operands)]), list(refs[len(operands) :])
            for kernel, taken, given in tasks:
                kernel(io, 0, (*inputs[: len(taken)], *results[: len(given)]))
                del inputs[: len(taken)], results[: len(given)]

        found = self.call(batch, 0, operands, outs, [], weight, ties)
        return [[found.pop(0) for _ in task[2]] for task in tasks]


def first_rows(parts, own):
    return functools.reduce(lambda a, b: a + b, [part[:own, :].astype(F32) for part in parts])


def group_last(io, many, refs):
    *parts, total = refs
    total[...] = first_rows(parts, total.shape[0]).astype(BF)


def add_rows(io, many, refs):
    *parts, total = refs
    rows = slice(total.shape[0], 2 * total.shape[0])
    total[...] = functools.reduce(
        lambda a, b: a + b, [part[rows, :].astype(F32) for part in parts]
    ).astype(BF)


def add_line(io, many, refs):
    own, came, carried = refs
    carried[...] = (own[...].astype(F32) + came[...].astype(F32)).astype(BF)


def exchange(part, bit, devices):
    return lax.ppermute(part, "dp", [(i, i ^ bit) for i in range(devices)])


def gather_group(own, count, devices):
    arrays, held, bit = [own], own, count // 2
    while bit:
        arrays.append(exchange(held, bit, devices))
        if bit > 1:
            held = jnp.concatenate([held, arrays[-1]], axis=0)
        bit //= 2
    return arrays


def gather_near(own, count, devices):
    arrays, bit = [own], 1
    while bit < count:
        held = jnp.concatenate(arrays, axis=0) if bit > 1 else own
        arrays.append(exchange(held, bit, devices))
        bit *= 2
    return arrays


def gather_rest(own, first, count, devices):
    arrays, bit = [own, *first], count // 4
    while bit:
        held = jnp.concatenate(arrays, axis=0)
        arrays.append(exchange(held, bit, devices))
        bit //= 2
    return arrays


class GroupSum:
    def __init__(self, keep, send, count, devices):
        self.arrays, self.to_send, self.bit = [keep], send, 1
        self.count, self.devices = count, devices

    def send(self):
        self.arrays.append(exchange(self.to_send, self.bit, self.devices))
        self.bit *= 2

    def done(self):
        return self.bit >= self.count

    def task(self):
        rows, columns = self.arrays[-1].shape
        return add_rows, self.arrays, [((rows // 2, columns), BF)]

    def take(self, found):
        (self.to_send,) = found

    def finish(self, order):
        while not self.done():
            self.take(*order.batch([self.task()], 1))
            self.send()


def add_parts(io, many, refs):
    kept_a, came_a, kept_b, came_b, send_a, keep_a, send_b, keep_b = refs
    cut, half = keep_a.shape[1], keep_a.shape[0]
    first = kept_b.shape[1] - keep_b.shape[1]

    def total(kept, came, index, rows):
        return (kept[index, rows, :].astype(F32) + came[index, rows, :].astype(F32)).astype(BF)

    for number in range(half):
        send_a[number] = total(kept_a, came_a, 2 * number + 1, slice(0, cut))
        keep_a[number] = total(kept_a, came_a, 2 * number, slice(0, cut))
        send_b[number] = total(kept_b, came_b, half + number, slice(first, None))
        keep_b[number] = total(kept_b, came_b, number, slice(first, None))


def add_last(io, many, refs):
    kept_a, came_a, kept_b, came_b, total = refs
    cut = kept_a.shape[1]
    total[:cut, :] = (kept_a[0].astype(F32) + came_a[0].astype(F32)).astype(BF)
    total[cut:, :] = (kept_b[0].astype(F32) + came_b[0].astype(F32)).astype(BF)


def add_two(io, many, refs):
    kept_a, came_a, kept_b, came_b, first, second = refs
    first[...] = (kept_a[0].astype(F32) + came_a[0].astype(F32)).astype(BF)
    second[...] = (kept_b[0].astype(F32) + came_b[0].astype(F32)).astype(BF)


class DpSum:
    def __init__(self, send, keep, devices):
        self.send, self.parts, self.devices = send, [keep], devices
        self.left = list(range(devices.bit_length() - 2))

    def step(self):
        if self.send is not None:
            total = self.parts[0] + exchange(self.send, 1, self.devices)
            cut = total.shape[1] // 32 * 16
            self.parts, self.send = [total[:, :cut], total[:, cut:]], None
            self.orders = [self.left[:], self.left[::-1]]
            return
        found = []
        for part, order in zip(self.parts, self.orders):
            bit = order[0]
            part = part.reshape(-1, 2, 1 << sorted(order).index(bit), *part.shape[1:])
            part = part[:, 0] + exchange(part[:, 1], 2 << bit, self.devices)
            part = part.reshape(-1, *part.shape[2:])
            order.remove(bit)
            found.append(part if order else part[0])
        self.parts, self.left = found, self.orders[0]


class LineSum:
    def __init__(self, own, count):
        self.parts, self.count, self.hop = [own, own, own], count, 0

    def step(self):
        self.hop += 1
        hop, count = self.hop, self.count
        total, own, carried = self.parts
        pairs = [(hop - 1, hop), (count - hop, count - hop - 1)]
        came = lax.ppermute(carried, "src", pairs)
        self.parts = [total + came, own, own + came]


def local(
    src_tok, src_ids, tgt_tok, tgt_ids, out_grad,
    enc_attn_in, enc_attn_out, enc_ffn_in, enc_ffn_out, enc_gains, enc_biases,
    dec_self_in, dec_self_out, dec_cross_q, dec_cross_kv, dec_cross_out,
    dec_ffn_in, dec_ffn_out, dec_gains, dec_biases,
):
    count, devices = lax.axis_size("src"), lax.axis_size("dp")
    _, own, features = src_tok.shape
    length = tgt_tok.shape[1]
    pairs = features // PAIR
    hidden = enc_ffn_in.shape[1]
    me, me_dp = lax.axis_index("src"), lax.axis_index("dp")
    turn = count // 2
    places = [row // 2 % turn if row % 2 == 0 else count - 1 - row // 2 % turn for row in range(devices)]
    inward = [
        (row * count + part, (row // 2 // turn * count + part) * count + places[row])
        for row in range(devices)
        for part in range(count)
    ]
    outward = [(there, here) for here, there in inward]

    def enter(a):
        return lax.ppermute(a, ("dp", "src"), inward)

    def leave(a):
        return lax.ppermute(a, ("dp", "src"), outward)

    def spread(arrays, offsets, bit):
        came = []
        for array, offset in zip(arrays, offsets):
            pairs = [
                ((row ^ offset) * count + there, (row ^ offset ^ bit) * count + there)
                for row, there in enumerate(places)
            ]
            came.append(lax.ppermute(array, ("dp", "src"), pairs))
        return came

    def holder():
        return sum(
            number * ((me == there) & (me_dp == row ^ offset))
            for row, there in enumerate(places)
            for number, offset in enumerate(spread_order(count))
        )

    first = me * own
    ids = jnp.concatenate([src_ids.reshape(count, own), tgt_ids.reshape(count, own)], axis=0)
    ids = jnp.pad(ids, ((0, ID_ROWS - 2 * count), (0, features - own))).astype(BF)
    source = enter(src_tok[0])
    names = enter(ids)
    source_first = exchange(source, count // 2, devices)
    names, source_first = lax.optimization_barrier((names, source_first))
    source_pieces = gather_rest(source, [source_first], count, devices)
    target, own_grad, source_pieces[-1] = lax.optimization_barrier(
        (tgt_tok[0], out_grad[0], source_pieces[-1])
    )
    own_grad = lax.dynamic_slice_in_dim(own_grad, first, own, 0)
    spreading, offsets, bit = [target], [0], count // 2
    spreading += spread(spreading, offsets, bit)
    which = holder()
    place = jnp.stack([lax.rem(me_dp, count), me_dp, which]).astype(jnp.int32)
    many = len(source_pieces)
    narrow, half = (own, features), (length // 2, features)
    shard = features // devices
    column = ((own, 1), F32)
    pair_stats = ((pairs, 2, own), F32)
    all_keys = ((length, 2 * features), BF)
    id_scratch = ((ID_ROWS, features), F32)
    bias_scratch = ((length, own), F32)
    small_product = ((devices, shard, features), BF)
    product = ((devices, hidden // devices, features), BF)

    def bucket(rows):
        return [((devices // 2, rows, features), BF)] * 2

    ffn_rows = 2 * shard * (hidden // features)

    order = Order(place)
    norm_columns = features + PAIR

    q_e, kv_e, stats_e, mixed_e, norms_e, memory = order.call(
        encoder_forward, many,
        [*map(Far, source_pieces), names, Far(enc_attn_in), Far(enc_attn_out), Far(enc_ffn_in), Far(enc_ffn_out), Far(enc_gains), Far(enc_biases)],
        [(narrow, BF, "far"), (*all_keys, "far"), (*pair_stats, "far"), (narrow, F32, "far"),
         ((own, 2 * norm_columns), F32, "far"), (narrow, BF)],
        [bias_scratch, id_scratch],
        11,
    )
    memory, spreading[-1] = lax.optimization_barrier((memory, spreading[-1]))
    memory_pieces = gather_near(memory, count, devices)
    offsets, bit = spread_order(count)[: len(spreading)], bit // 2
    while bit:
        spreading += spread(spreading, offsets, bit)
        offsets, bit = spread_order(count)[: len(spreading)], bit // 2
    target = Choice([a.reshape(count, own, features) for a in spreading])
    own_grad = enter(own_grad)
    q_d, kv_d, stats_d, mixed_d, norms_d = order.call(
        decoder_self_forward, many,
        [target, names, Far(dec_self_in), Far(dec_self_out)],
        [(narrow, BF, "far"), (*all_keys, "far"), (*pair_stats, "far"), (narrow, F32, "far"),
         ((own, norm_columns), F32)],
        [bias_scratch, id_scratch],
        9,
    )
    early_rows = ffn_rows + 4 * shard
    shards, out_own, memory_keep, memory_send, d_target, vectors_d = order.call(
        decoder_middle, many,
        [*memory_pieces, names, norms_d, own_grad, Far(dec_cross_q), Far(dec_cross_kv),
         Far(dec_cross_out), Far(dec_ffn_in), Far(dec_ffn_out), Far(dec_gains), Far(dec_biases)],
        [((devices, early_rows, features), BF, "far"), (narrow, BF, "far"), (half, BF), (half, BF),
         (narrow, F32), ((6, features), F32, "far")],
        [bias_scratch, id_scratch, (narrow, BF), all_keys, pair_stats, (narrow, F32), (narrow, BF),
         (narrow, BF), all_keys, ((length, features), BF)],
        28,
    )
    early = lax.psum_scatter(shards, "dp", scatter_dimension=0, tiled=True)[0]
    memory_sum = GroupSum(memory_keep, memory_send, count, devices)
    memory_sum.send()
    memory_sum.finish(order)
    target_keep, target_send, pack_d, dkv_d = order.call(
        decoder_self_back, many,
        [d_target, names, Far(q_d), Far(kv_d), Far(stats_d), Far(mixed_d), Far(dec_self_in),
         Far(dec_self_out)],
        [(half, BF), (half, BF), ((3 * own, features), BF, "far"), (*all_keys, "far")],
        [bias_scratch, id_scratch, (narrow, BF), (narrow, BF)],
        14,
    )
    target_sum = GroupSum(target_keep, target_send, count, devices)
    target_sum.send()
    d_source, vectors_e, pack_f, wide_f = order.call(
        encoder_ffn_back, len(memory_sum.arrays),
        [*memory_sum.arrays, Far(norms_e), Far(enc_ffn_in), Far(enc_ffn_out), Far(enc_gains),
         Far(enc_biases)],
        [(narrow, F32), ((4, features), F32, "far"), ((2 * own, features), BF, "far"),
         ((own, 2 * hidden), BF, "far")],
        [],
        7,
    )
    (target_sum.to_send,), (out_own,) = order.batch(
        [target_sum.task(), (group_last, [out_own], [(narrow, BF)])], 2
    )
    out_back = leave(out_own)
    target_sum.send()
    target_sum.finish(order)
    source_keep, source_send, pack_e, dkv_e = order.call(
        encoder_attention_back, many,
        [d_source, names, Far(q_e), Far(kv_e), Far(stats_e), Far(mixed_e), Far(enc_attn_in),
         Far(enc_attn_out)],
        [(half, BF), (half, BF), ((3 * own, features), BF, "far"), (*all_keys, "far")],
        [bias_scratch, id_scratch, (narrow, BF), (narrow, BF)],
        14,
    )
    source_sum = GroupSum(source_keep, source_send, count, devices)
    source_sum.send()
    send_s, keep_s, send_u, keep_u = order.call(
        late_weights, many,
        [*map(Far, source_pieces), target,
         *map(Far, [pack_d, dkv_d, pack_f, wide_f, pack_e, dkv_e, vectors_d, vectors_e])],
        bucket(8 * shard + VECTOR_ROWS) + bucket(ffn_rows),
        [product, ((length, features), BF)],
        10, [*target_sum.arrays[1:], out_back],
    )
    back = leave(first_rows(target_sum.arrays, own).astype(BF))
    sums = [DpSum(send, keep, devices) for send, keep in ((send_s, keep_s), (send_u, keep_u))]
    for one in sums:
        one.step()
    early, back, out_back, *flat = lax.optimization_barrier(
        (early, back, out_back, *source_sum.arrays, *(p for one in sums for p in one.parts))
    )
    source_sum.arrays = flat[: len(source_sum.arrays)]
    del flat[: len(source_sum.arrays)]
    early = LineSum(early, count)
    early.step()
    dec_out, tgt_grad = (
        lax.all_gather(a, "src", axis=0, tiled=True) for a in (out_back, back)
    )
    while not source_sum.done():
        rows = source_sum.arrays[-1].shape[0] // 2
        source_sum.to_send = first_rows([a[rows:] for a in source_sum.arrays], rows).astype(BF)
        source_sum.send()
    for one in sums:
        one.parts = [flat.pop(0) for _ in one.parts]
        one.step()
    src_grad = leave(first_rows(source_sum.arrays, own).astype(BF))
    flat = (early.parts, src_grad, dec_out, *(p for one in sums for p in one.parts))
    early.parts, src_grad, dec_out, *flat = lax.optimization_barrier(flat)
    src_grad = src_grad.astype(F32)
    early.step()
    for one in sums:
        one.parts = [flat.pop(0) for _ in one.parts]
        while one.left:
            one.step()
    flat = [p for one in sums for p in one.parts]
    early.parts, *flat = lax.optimization_barrier((early.parts, *flat))
    flat = [jnp.concatenate(flat[i : i + 2], axis=0) for i in (0, 2)]
    lines = [LineSum(one, count) for one in flat] + [early]
    while any(line.hop < count - 1 for line in lines):
        for line in lines:
            if line.hop < count - 1:
                line.step()
    *sums, early = (line.parts[0].astype(F32) for line in lines)
    tgt_grad = tgt_grad.astype(F32)
    selfs, ffn_e = sums
    self_d, attn_e = selfs[: 4 * shard], selfs[4 * shard :]
    ffn_d, cross = early[:ffn_rows], early[ffn_rows:]

    def wide(rows):
        return jnp.concatenate(jnp.split(rows, rows.shape[0] // shard, axis=0), axis=1)

    up = shard * (hidden // features)
    vectors = attn_e[4 * shard :]
    vectors = lax.dynamic_slice_in_dim(vectors, me_dp * shard, shard, 1)
    return (
        dec_out[None],
        src_grad[None],
        tgt_grad[None],
        wide(attn_e[: 3 * shard]),
        attn_e[3 * shard : 4 * shard],
        wide(ffn_e[:up]),
        ffn_e[up:],
        jnp.stack([vectors[8], vectors[6]]),
        jnp.stack([vectors[9], vectors[7]]),
        wide(self_d[: 3 * shard]),
        self_d[3 * shard :],
        cross[shard : 2 * shard],
        wide(cross[2 * shard :]),
        cross[:shard],
        wide(ffn_d[:up]),
        ffn_d[up:],
        jnp.stack([vectors[4], vectors[2], vectors[0]]),
        jnp.stack([vectors[5], vectors[3], vectors[1]]),
    )


def solution(mesh):
    row, part = P("dp", None, None), P("dp", "src", None)
    line, rows, columns = P("dp", None), P("dp", None), P(None, "dp")
    in_specs = (part, line, row, line, row) + (P(),) * 15
    out_specs = (
        row, part, row, rows, rows, rows, rows, columns, columns,
        rows, rows, rows, rows, rows, rows, rows, columns, columns,
    )
    return jax.shard_map(local, mesh=mesh, in_specs=in_specs, out_specs=out_specs, check_vma=False)
```

```python
import functools
import math

import jax
import jax.numpy as jnp
from jax import lax
from jax.experimental import pallas as pl
from jax.experimental.pallas import tpu as pltpu
from jax.sharding import PartitionSpec as P

HEAD_DIM = 64
PAIR = 2 * HEAD_DIM
EPS = 1e-05
NEGATIVE = -1e30
BF = jnp.bfloat16
F32 = jnp.float32
BLOCK = 1024
VECTOR_ROWS = 32
ID_ROWS = 16
LIMIT = 34


def dot(former, latter, dims):
    return lax.dot_general(former, latter, (dims, ((), ())), preferred_element_type=F32)


def nn(former, latter):
    return dot(former, latter, ((1,), (0,)))


def nt(former, latter):
    return dot(former, latter, ((1,), (1,)))


def tn(former, latter):
    return dot(former, latter, ((0,), (0,)))


def norm(v):
    centred = v - jnp.mean(v, axis=-1, keepdims=True)
    inverse = lax.rsqrt(jnp.mean(centred * centred, axis=-1, keepdims=True) + EPS)
    return centred * inverse, inverse


def norm_back(du, normed, inverse, gain):
    gain_grad = jnp.sum(du * normed, axis=0, keepdims=True)
    bias_grad = jnp.sum(du, axis=0, keepdims=True)
    scaled = du * gain
    mean = jnp.mean(scaled, axis=-1, keepdims=True)
    slope = jnp.mean(scaled * normed, axis=-1, keepdims=True)
    return inverse * (scaled - mean - normed * slope), gain_grad, bias_grad


def head_halves(pair, scale):
    wide = pair.astype(F32) * scale
    first = lax.broadcasted_iota(jnp.int32, wide.shape, 1) < HEAD_DIM
    return [jnp.where(first, wide, 0.0).astype(BF), jnp.where(first, 0.0, wide).astype(BF)]


def pair_columns(pair, offset=0):
    return pl.ds(pl.multiple_of(pair * PAIR + offset, PAIR), PAIR)


def mask_bias(key_ids, query_ids):
    return jnp.where(key_ids == query_ids, 0.0, NEGATIVE)


def pair_forward(q, k, v, bias):
    queries = head_halves(q, HEAD_DIM**-0.5)
    values = v.T
    mixed, stats = [], []
    for head in range(2):
        s = nt(k, queries[head]) + bias
        maximum = jnp.max(s, axis=0, keepdims=True)
        e = jnp.exp(s - maximum)
        total = jnp.sum(e, axis=0, keepdims=True)
        o = nn(values[head * HEAD_DIM : (head + 1) * HEAD_DIM], e.astype(BF))
        mixed.append(o * (1.0 / total))
        stats.append(maximum + jnp.log(total))
    return jnp.concatenate(mixed, axis=0).T, jnp.concatenate(stats, axis=0)


def pair_delta(o, grad):
    product = (o * grad.astype(F32)).T
    return (
        jnp.sum(product[:HEAD_DIM], axis=0, keepdims=True),
        jnp.sum(product[HEAD_DIM:], axis=0, keepdims=True),
    )


def block_backward(qs, gs, k, v, keys, bias, stats, deltas):
    dq, dk, dv = [], None, None
    for head in range(2):
        s = nt(k, qs[head]) + bias
        p = jnp.exp(s - stats[head : head + 1])
        ds = (p * (nt(v, gs[head]) - deltas[head])).astype(BF)
        p = p.astype(BF)
        dq.append(nn(keys[head * HEAD_DIM : (head + 1) * HEAD_DIM], ds))
        dk_term, dv_term = nn(ds, qs[head]), nn(p, gs[head])
        dk = dk_term if dk is None else dk + dk_term
        dv = dv_term if dv is None else dv + dv_term
    return jnp.concatenate(dq, axis=0), dk, dv


def cross_backward(q_ref, kv_ref, o_ref, g_ref, bias_ref, stats_ref, dq_ref, dkv_ref):
    features = q_ref.shape[1]
    keys_count = kv_ref.shape[0]

    def one_pair(pair, carry):
        columns = pair_columns(pair)
        value_columns = pair_columns(pair, features)
        q, g = q_ref[:, columns], g_ref[:, columns]
        qs = head_halves(q, HEAD_DIM**-0.5)
        gs = head_halves(g, 1.0)
        deltas = pair_delta(o_ref[:, columns], g)
        stats = stats_ref[pair]
        total = None
        for first in range(0, keys_count, BLOCK):
            rows = slice(first, first + BLOCK)
            k = kv_ref[rows, columns]
            term, dk, dv = block_backward(
                qs, gs, k, kv_ref[rows, value_columns], k.T, bias_ref[rows, :], stats, deltas
            )
            dkv_ref[rows, columns] = dk.astype(BF)
            dkv_ref[rows, value_columns] = dv.astype(BF)
            total = term if total is None else total + term
        dq_ref[:, columns] = (total.T * HEAD_DIM**-0.5).astype(BF)
        return carry

    lax.fori_loop(0, features // PAIR, one_pair, 0)


def emit(me_dp, product, former, latter, send, keep, offset):
    devices = 2 * send.shape[0]
    width = product.shape[2]
    height = former.shape[1]
    rows = height // devices
    for first in range(0, latter.shape[1], width):
        term = tn(former, latter[:, first : first + width]).astype(BF)
        product[:, :rows, :] = term.reshape(devices, rows, width)
        for slot in range(devices):
            target = send if slot % 2 else keep
            target[slot // 2, offset : offset + rows, :] = product[
                jnp.bitwise_xor(me_dp, slot), :rows, :
            ]
        offset += rows
    return offset


def sigmoid(v):
    return 1.0 / (1.0 + jnp.exp(-v))


def silu_parts(pre):
    squashed = sigmoid(pre)
    return pre * squashed, squashed * (1.0 + pre * (1.0 - squashed))


def near_order(count):
    order, bit = [0], 1
    while bit < count:
        order += [o ^ bit for o in order]
        bit *= 2
    return order


def near_blocks(refs, own, count):
    found = blocks_of(refs, own, own)
    return [found[near_order(count).index(o)] for o in key_order(count)]


def blocks_of(refs, height, own):
    found = []
    for ref in refs:
        for first in range(0, ref.shape[0], height):
            found.append((ref, slice(first, first + own)))
    return found


def key_order(count):
    order = [0]
    bit = count // 2
    while bit:
        order += [o ^ bit for o in order]
        bit //= 2
    return order


def spread_order(count):
    order, bit = [0], count // 2
    while bit:
        order += [o ^ bit for o in order]
        bit //= 2
    return order


def fill_bias(bias, ids, first_key, first_query, member, causal):
    keys_count, own = bias.shape
    count = keys_count // own
    lines = ids[:, :own]
    numbers = lax.broadcasted_iota(jnp.int32, lines.shape, 0)

    def pick(row):
        return jnp.sum(jnp.where(numbers == row, lines, 0.0), axis=0, keepdims=True)

    queries = pick(first_query + member)
    for number, offset in enumerate(key_order(count)):
        peer = jnp.bitwise_xor(member, offset)
        line = jnp.broadcast_to(pick(first_key + peer), (128, own)).T
        line = jnp.concatenate([line] * (own // 128), axis=1)
        term = mask_bias(line, queries)
        if causal:
            keys = lax.broadcasted_iota(jnp.int32, term.shape, 0) + (peer - member) * own
            term = jnp.where(keys <= lax.broadcasted_iota(jnp.int32, term.shape, 1), term, NEGATIVE)
        bias[number * own : (number + 1) * own, :] = term


def attend(q, kv, bias, mixed, stats):
    features = q.shape[1]

    def one_pair(pair, carry):
        columns = pair_columns(pair)
        o, logsum = pair_forward(
            q[:, columns], kv[:, columns], kv[:, pair_columns(pair, features)], bias[...]
        )
        mixed[:, columns] = o
        stats[pair] = logsum
        return carry

    lax.fori_loop(0, features // PAIR, one_pair, 0)


def project(blocks, weight, columns, target):
    for number, (ref, rows) in enumerate(blocks):
        own = rows.stop - rows.start
        target[number * own : (number + 1) * own, :] = nn(ref[rows, :], weight[:, columns]).astype(BF)


def put_norm(target, number, normed, inverse):
    features = normed.shape[1]
    count = target.shape[1] // (features + PAIR)
    target[:, number * features : (number + 1) * features] = normed
    first = count * features + number * PAIR
    target[:, first : first + PAIR] = jnp.broadcast_to(inverse, (inverse.shape[0], PAIR))


def get_norm(source, number, features):
    count = source.shape[1] // (features + PAIR)
    first = count * features + number * PAIR
    return source[:, number * features : (number + 1) * features], source[:, first : first + 1]


def encoder_forward(io, many, refs):
    pieces = refs[:many]
    (names, w_in, w_out, w_up, w_down, gains, biases,
     q, kv, stats, mixed, norms, memory, bias, ids) = refs[many:]
    own, features = q.shape
    blocks = blocks_of(pieces, own, own)
    io.ready(pieces[0], w_in)
    q[...] = nn(pieces[0][...], w_in[:, :features]).astype(BF)
    io.ready(*pieces)
    project(blocks, w_in, slice(features, 3 * features), kv)
    ids[...] = names[...].astype(F32)
    fill_bias(bias, ids, 0, 0, io.place[0], False)
    attend(q, kv, bias, mixed, stats)
    io.flush(q, kv, stats, mixed)
    io.ready(w_out, gains, biases, w_up, w_down)
    v = pieces[0][...].astype(F32) + nn(mixed[...].astype(BF), w_out[...])
    normed, inverse = norm(v)
    put_norm(norms, 0, normed, inverse)
    x1 = normed * gains[0:1, :] + biases[0:1, :]
    pre = nn(x1.astype(BF), w_up[...])
    hidden = (pre * sigmoid(pre)).astype(BF)
    normed, inverse = norm(x1 + nn(hidden, w_down[...]))
    put_norm(norms, 1, normed, inverse)
    memory[...] = (normed * gains[1:2, :] + biases[1:2, :]).astype(BF)


def decoder_self_forward(io, many, refs):
    tokens, names, w_in, w_out, q, kv, stats, mixed, norms, bias, ids = refs
    own, features = q.shape
    count = tokens.shape[0]
    member = io.place[0]
    io.ready(names, tokens, w_in)
    ids[...] = names[...].astype(F32)
    mine = tokens[member]
    q[...] = nn(mine, w_in[:, :features]).astype(BF)
    for number, offset in enumerate(key_order(count)):
        kv[number * own : (number + 1) * own, :] = nn(
            tokens[jnp.bitwise_xor(member, offset)], w_in[:, features:]
        ).astype(BF)
    fill_bias(bias, ids, count, count, member, True)
    attend(q, kv, bias, mixed, stats)
    io.flush(q, kv, stats, mixed)
    io.ready(w_out)
    normed, inverse = norm(mine.astype(F32) + nn(mixed[...].astype(BF), w_out[...]))
    put_norm(norms, 0, normed, inverse)


def decoder_middle(io, many, refs):
    pieces = refs[:many]
    (names, norms, out_grad, w_q, w_kv, w_out, w_up, w_down, gains, biases,
     shards, dec_out, memory_keep, memory_send, d_target, vectors,
     bias, ids, q, kv, stats, mixed, dq, grad, dkv, memory) = refs[many:]
    own, features = q.shape
    count = kv.shape[0] // own
    half = memory_keep.shape[0]
    io.ready(names, norms, gains, biases, w_q)
    ids[...] = names[...].astype(F32)
    normed_c, inverse_c = get_norm(norms, 0, features)
    y1 = normed_c * gains[0:1, :] + biases[0:1, :]
    y1_low = y1.astype(BF)
    q[...] = nn(y1_low, w_q[...]).astype(BF)
    io.ready(w_kv, *pieces)
    project(near_blocks(pieces, own, count), w_kv, slice(None), kv)
    fill_bias(bias, ids, 0, count, io.place[0], False)
    attend(q, kv, bias, mixed, stats)
    io.ready(w_out, w_up, w_down, out_grad)
    mixed_low = mixed[...].astype(BF)
    normed_d, inverse_d = norm(y1 + nn(mixed_low, w_out[...]))
    y2 = normed_d * gains[1:2, :] + biases[1:2, :]
    y2_low = y2.astype(BF)
    act, slope = silu_parts(nn(y2_low, w_up[...]))
    hidden = act.astype(BF)
    normed, inverse = norm(y2 + nn(hidden, w_down[...]))
    dec_out[...] = (normed * gains[2:3, :] + biases[2:3, :]).astype(BF)
    dv, gain_grad, bias_grad = norm_back(
        out_grad[...].astype(F32), normed, inverse, gains[2:3, :]
    )
    vectors[0:1, :] = gain_grad
    vectors[1:2, :] = bias_grad
    dv_low = dv.astype(BF)
    d_pre = (nt(dv_low, w_down[...]) * slope).astype(BF)
    devices, _, width = shards.shape
    offset = 0

    def emit_all(former, latter, offset):
        rows = former.shape[1] // devices
        for first in range(0, latter.shape[1], width):
            term = tn(former, latter[:, first : first + width]).astype(BF)
            shards[:, offset : offset + rows, :] = term.reshape(devices, rows, width)
            offset += rows
        return offset

    offset = emit_all(y2_low, d_pre, offset)
    offset = emit_all(hidden, dv_low, offset)
    io.flush(dec_out)
    d_second = dv + nt(d_pre, w_up[...])
    dv, gain_grad, bias_grad = norm_back(d_second, normed_d, inverse_d, gains[1:2, :])
    vectors[2:3, :] = gain_grad
    vectors[3:4, :] = bias_grad
    dv_low = dv.astype(BF)
    offset = emit_all(mixed_low, dv_low, offset)
    grad[...] = nt(dv_low, w_out[...]).astype(BF)
    cross_backward(q, kv, mixed, grad, bias, stats, dq, dkv)
    offset = emit_all(y1_low, dq[...], offset)
    emit_all(whole(near_blocks(pieces, own, count), memory), dkv[...], offset)
    io.flush(shards)
    memory_send[...] = nt(dkv[half:, :], w_kv[...]).astype(BF)
    memory_keep[...] = nt(dkv[:half, :], w_kv[...]).astype(BF)
    io.flush(memory_send, memory_keep)
    d_first = dv + nt(dq[...], w_q[...])
    dv, gain_grad, bias_grad = norm_back(d_first, normed_c, inverse_c, gains[0:1, :])
    vectors[4:5, :] = gain_grad
    vectors[5:6, :] = bias_grad
    d_target[...] = dv


def whole(blocks, target):
    for number, (ref, rows) in enumerate(blocks):
        own = rows.stop - rows.start
        target[number * own : (number + 1) * own, :] = ref[rows, :]
    return target[...]


def self_back(io, refs, first_id, causal):
    (dv, names, q, kv, stats, mixed, w_in, w_out, keep, send, pack, dkv, bias, ids, grad, dq) = refs
    own, features = q.shape
    half = keep.shape[0]
    io.ready(names, dv, mixed, w_out)
    ids[...] = names[...].astype(F32)
    fill_bias(bias, ids, first_id, first_id, io.place[0], causal)
    dv_low = dv[...].astype(BF)
    pack[own : 2 * own, :] = dv_low
    pack[2 * own :, :] = mixed[...].astype(BF)
    grad[...] = nt(dv_low, w_out[...]).astype(BF)
    io.ready(q, kv, stats)
    cross_backward(q, kv, mixed, grad, bias, stats, dq, dkv)
    pack[:own, :] = dq[...]
    io.flush(pack, dkv)
    io.ready(w_in)
    send[...] = nt(dkv[half:, :], w_in[:, features:]).astype(BF)
    io.flush(send)
    term = nt(dkv[:half, :], w_in[:, features:])
    keep[own:, :] = term[own:].astype(BF)
    keep[:own, :] = (term[:own] + dv[...] + nt(dq[...], w_in[:, :features])).astype(BF)


def decoder_self_back(io, many, refs):
    q, kv = refs[2:4]
    self_back(io, refs, kv.shape[0] // q.shape[0], True)


def encoder_attention_back(io, many, refs):
    self_back(io, refs, 0, False)


def emit_self(io, tokens, pack, dkv, send, keep, product, offset):
    own = pack.shape[0] // 3
    offset = emit(io.place[1], product, tokens[:own, :], pack[:own, :], send, keep, offset)
    offset = emit(io.place[1], product, tokens[...], dkv[...], send, keep, offset)
    return emit(
        io.place[1], product, pack[2 * own :, :], pack[own : 2 * own, :], send, keep, offset
    )


def encoder_ffn_back(io, many, refs):
    d_memory = refs[:many]
    norms, w_up, w_down, gains, biases, d_source, vectors, send, keep, product = refs[many:]
    own, features = d_source.shape
    io.ready(*d_memory, norms, gains, biases)
    du = first_rows(d_memory, own)
    dv, gain_grad, bias_grad = norm_back(du, *get_norm(norms, 1, features), gains[1:2, :])
    vectors[0:1, :] = gain_grad
    vectors[1:2, :] = bias_grad
    dv_low = dv.astype(BF)
    normed_a, inverse_a = get_norm(norms, 0, features)
    x1_low = (normed_a * gains[0:1, :] + biases[0:1, :]).astype(BF)
    io.ready(w_up, w_down)
    act, slope = silu_parts(nn(x1_low, w_up[...]))
    hidden = act.astype(BF)
    d_pre = (nt(dv_low, w_down[...]) * slope).astype(BF)
    offset = emit(io.place[1], product, x1_low, d_pre, send, keep, 0)
    emit(io.place[1], product, hidden, dv_low, send, keep, offset)
    d_mid = dv + nt(d_pre, w_up[...])
    dv, gain_grad, bias_grad = norm_back(d_mid, normed_a, inverse_a, gains[0:1, :])
    vectors[2:3, :] = gain_grad
    vectors[3:4, :] = bias_grad
    d_source[...] = dv


def late_weights(io, many, refs):
    pieces = refs[:many]
    (tokens, pack_d, dkv_d, pack_e, dkv_e, vectors_d, vectors_e,
     send, keep, product, ordered) = refs[many:]
    count, own, features = tokens.shape
    io.ready(tokens, pack_d, dkv_d)
    for number, peer in enumerate(key_order(count)):
        rows = slice(number * own, (number + 1) * own)
        ordered[rows, :] = tokens[jnp.bitwise_xor(io.place[0], peer)]
    offset = emit_self(io, ordered, pack_d, dkv_d, send, keep, product, 0)
    io.ready(*pieces, pack_e, dkv_e, vectors_d, vectors_e)
    whole(blocks_of(pieces, own, own), ordered)
    offset = emit_self(io, ordered, pack_e, dkv_e, send, keep, product, offset)
    rows = jnp.concatenate(
        [vectors_d[...], vectors_e[...], jnp.zeros((VECTOR_ROWS - 10, features), F32)], axis=0
    ).astype(BF)
    for slot in range(send.shape[0]):
        send[slot, offset : offset + VECTOR_ROWS, :] = rows
        keep[slot, offset : offset + VECTOR_ROWS, :] = rows


class Far:
    def __init__(self, array):
        self.array = array


class Choice:
    def __init__(self, arrays):
        self.arrays = arrays


class ChosenCopy:
    def __init__(self, place, sources, target, semaphore):
        self.which = place[2]
        self.copies = [pltpu.make_async_copy(a, target, semaphore) for a in sources]

    def start(self):
        for number, copy in enumerate(self.copies):
            pl.when(self.which == number)(copy.start)

    def wait(self):
        self.copies[0].wait()


class Io:
    def __init__(self, place, arriving, leaving):
        self.place, self.arriving, self.leaving, self.gone = place, arriving, leaving, []
        for copy in arriving.values():
            copy.start()

    def ready(self, *refs):
        for ref in refs:
            copy = self.arriving.pop(id(ref), None)
            if copy is not None:
                copy.wait()

    def flush(self, *refs):
        for ref in refs:
            copy = self.leaving.pop(id(ref), None)
            if copy is not None:
                copy.start()
                self.gone.append(copy)

    def finish(self):
        for copy in self.arriving.values():
            copy.wait()
        for copy in self.leaving.values():
            copy.start()
        for copy in [*self.gone, *self.leaving.values()]:
            copy.wait()


class Order:
    def __init__(self, place):
        self.place = place

    def run(self, body, name, operands, outs, in_specs, out_specs, scratch, weight, grid=()):
        moved = sum(math.prod(a.shape) * a.dtype.itemsize for a in (*operands, *outs))
        found = pl.pallas_call(
            body,
            name=name,
            grid=grid,
            out_shape=[jax.ShapeDtypeStruct((3,), jnp.int32), *outs],
            in_specs=[pl.BlockSpec(memory_space=pltpu.SMEM), *in_specs],
            out_specs=[pl.BlockSpec(memory_space=pltpu.SMEM), *out_specs],
            scratch_shapes=scratch,
            compiler_params=pltpu.CompilerParams(vmem_limit_bytes=LIMIT * 1024 * 1024),
            cost_estimate=pl.CostEstimate(
                flops=int(weight * 1.15e9), bytes_accessed=int(moved), transcendentals=0
            ),
        )(self.place, *operands)
        self.place = found[0]
        return list(found[1:])

    def call(self, kernel, many, operands, outs, scratch, weight, ties=()):
        far_out = [i for i, out in enumerate(outs) if len(out) == 3]
        groups, flat, spaces, held = [], [], [], []
        for a in operands:
            if isinstance(a, (Far, Choice)):
                arrays = a.arrays if isinstance(a, Choice) else [a.array]
                held.append(arrays[0])
                arrays = [pltpu.with_memory_space_constraint(one, pltpu.HBM) for one in arrays]
                space = pltpu.HBM
            else:
                arrays, space = [a], pltpu.VMEM
            groups.append((slice(len(flat), len(flat) + len(arrays)), space == pltpu.HBM))
            flat += arrays
            spaces += [pl.BlockSpec(memory_space=space)] * len(arrays)
        outs = [jax.ShapeDtypeStruct(*out[:2]) for out in outs]
        count, tied, far_in = len(flat), len(ties), len(held)

        def wrapped(place, *refs):
            sources, refs = refs[:count], refs[count + tied :]
            after, results, refs = refs[0], list(refs[1 : 1 + len(outs)]), refs[1 + len(outs) :]
            here, refs = list(refs[:far_in]), refs[far_in:]
            inputs, arriving, leaving = [], {}, {}
            for places, far in groups:
                if far:
                    target = here[len(arriving)]
                    semaphore = refs[-2].at[len(arriving)]
                    arriving[id(target)] = ChosenCopy(place, sources[places], target, semaphore)
                    if places.stop - places.start == 1:
                        arriving[id(target)] = arriving[id(target)].copies[0]
                    inputs.append(target)
                else:
                    inputs.append(sources[places.start])
            for number, i in enumerate(far_out):
                target = refs[number]
                leaving[id(target)] = pltpu.make_async_copy(target, results[i], refs[-1].at[number])
                results[i] = target
            refs = refs[len(far_out) : -2]
            for i in range(3):
                after[i] = place[i]
            io = Io(place, arriving, leaving)
            kernel(io, many, (*inputs, *results, *refs))
            io.finish()

        held += [outs[i] for i in far_out]
        out_specs = [
            pl.BlockSpec(memory_space=pltpu.HBM if i in far_out else pltpu.VMEM)
            for i in range(len(outs))
        ]
        outs = [pltpu.HBM(a.shape, a.dtype) if i in far_out else a for i, a in enumerate(outs)]
        return self.run(
            wrapped, kernel.__name__, [*flat, *ties], outs,
            spaces + [pl.BlockSpec(memory_space=pl.ANY)] * tied, out_specs,
            [pltpu.VMEM(a.shape, a.dtype) for a in held]
            + [pltpu.VMEM(shape, dtype) for shape, dtype in scratch]
            + [pltpu.SemaphoreType.DMA((max(1, n),)) for n in (far_in, len(far_out))],
            weight,
        )

    def batch(self, tasks, weight, ties=()):
        operands = [a for task in tasks for a in task[1]]
        outs = [out for task in tasks for out in task[2]]

        def batch(io, many, refs):
            inputs, results = list(refs[: len(operands)]), list(refs[len(operands) :])
            for kernel, taken, given in tasks:
                kernel(io, 0, (*inputs[: len(taken)], *results[: len(given)]))
                del inputs[: len(taken)], results[: len(given)]

        found = self.call(batch, 0, operands, outs, [], weight, ties)
        return [[found.pop(0) for _ in task[2]] for task in tasks]


def first_rows(parts, own):
    return functools.reduce(lambda a, b: a + b, [part[:own, :].astype(F32) for part in parts])


def group_last(io, many, refs):
    *parts, total = refs
    total[...] = first_rows(parts, total.shape[0]).astype(BF)


def add_rows(io, many, refs):
    *parts, total = refs
    rows = slice(total.shape[0], 2 * total.shape[0])
    total[...] = functools.reduce(
        lambda a, b: a + b, [part[rows, :].astype(F32) for part in parts]
    ).astype(BF)


def add_line(io, many, refs):
    own, came, carried = refs
    carried[...] = (own[...].astype(F32) + came[...].astype(F32)).astype(BF)


def exchange(part, bit, devices):
    return lax.ppermute(part, "dp", [(i, i ^ bit) for i in range(devices)])


def gather_group(own, count, devices):
    arrays, held, bit = [own], own, count // 2
    while bit:
        arrays.append(exchange(held, bit, devices))
        if bit > 1:
            held = jnp.concatenate([held, arrays[-1]], axis=0)
        bit //= 2
    return arrays


def gather_near(own, count, devices):
    arrays, bit = [own], 1
    while bit < count:
        held = jnp.concatenate(arrays, axis=0) if bit > 1 else own
        arrays.append(exchange(held, bit, devices))
        bit *= 2
    return arrays


def gather_rest(own, first, count, devices):
    arrays, bit = [own, *first], count // 4
    while bit:
        held = jnp.concatenate(arrays, axis=0)
        arrays.append(exchange(held, bit, devices))
        bit //= 2
    return arrays


class GroupSum:
    def __init__(self, keep, send, count, devices):
        self.arrays, self.to_send, self.bit = [keep], send, 1
        self.count, self.devices = count, devices

    def send(self):
        self.arrays.append(exchange(self.to_send, self.bit, self.devices))
        self.bit *= 2

    def done(self):
        return self.bit >= self.count

    def task(self):
        rows, columns = self.arrays[-1].shape
        return add_rows, self.arrays, [((rows // 2, columns), BF)]

    def take(self, found):
        (self.to_send,) = found

    def finish(self, order):
        while not self.done():
            self.take(*order.batch([self.task()], 1))
            self.send()


def add_parts(io, many, refs):
    kept_a, came_a, kept_b, came_b, send_a, keep_a, send_b, keep_b = refs
    cut, half = keep_a.shape[1], keep_a.shape[0]
    first = kept_b.shape[1] - keep_b.shape[1]

    def total(kept, came, index, rows):
        return (kept[index, rows, :].astype(F32) + came[index, rows, :].astype(F32)).astype(BF)

    for number in range(half):
        send_a[number] = total(kept_a, came_a, 2 * number + 1, slice(0, cut))
        keep_a[number] = total(kept_a, came_a, 2 * number, slice(0, cut))
        send_b[number] = total(kept_b, came_b, half + number, slice(first, None))
        keep_b[number] = total(kept_b, came_b, number, slice(first, None))


def add_last(io, many, refs):
    kept_a, came_a, kept_b, came_b, total = refs
    cut = kept_a.shape[1]
    total[:cut, :] = (kept_a[0].astype(F32) + came_a[0].astype(F32)).astype(BF)
    total[cut:, :] = (kept_b[0].astype(F32) + came_b[0].astype(F32)).astype(BF)


def add_two(io, many, refs):
    kept_a, came_a, kept_b, came_b, first, second = refs
    first[...] = (kept_a[0].astype(F32) + came_a[0].astype(F32)).astype(BF)
    second[...] = (kept_b[0].astype(F32) + came_b[0].astype(F32)).astype(BF)


class DpSum:
    def __init__(self, send, keep, devices):
        self.send, self.parts, self.devices = send, [keep], devices
        self.left = list(range(devices.bit_length() - 2))

    def step(self):
        if self.send is not None:
            total = self.parts[0] + exchange(self.send, 1, self.devices)
            cut = total.shape[1] // 32 * 16
            self.parts, self.send = [total[:, :cut], total[:, cut:]], None
            self.orders = [self.left[:], self.left[::-1]]
            return
        found = []
        for part, order in zip(self.parts, self.orders):
            bit = order[0]
            part = part.reshape(-1, 2, 1 << sorted(order).index(bit), *part.shape[1:])
            part = part[:, 0] + exchange(part[:, 1], 2 << bit, self.devices)
            part = part.reshape(-1, *part.shape[2:])
            order.remove(bit)
            found.append(part if order else part[0])
        self.parts, self.left = found, self.orders[0]


def fence(*arrays):
    return lax.optimization_barrier(arrays)


class LineSum:
    def __init__(self, own, count):
        self.parts, self.count, self.hop = [own, own, own], count, 0

    def step(self):
        self.hop += 1
        hop, count = self.hop, self.count
        total, own, carried = self.parts
        pairs = [(hop - 1, hop), (count - hop, count - hop - 1)]
        came = lax.ppermute(carried, "src", pairs)
        self.parts = [total + came, own, own + came]


def local(
    src_tok, src_ids, tgt_tok, tgt_ids, out_grad,
    enc_attn_in, enc_attn_out, enc_ffn_in, enc_ffn_out, enc_gains, enc_biases,
    dec_self_in, dec_self_out, dec_cross_q, dec_cross_kv, dec_cross_out,
    dec_ffn_in, dec_ffn_out, dec_gains, dec_biases,
):
    count, devices = lax.axis_size("src"), lax.axis_size("dp")
    _, own, features = src_tok.shape
    length = tgt_tok.shape[1]
    pairs = features // PAIR
    hidden = enc_ffn_in.shape[1]
    me, me_dp = lax.axis_index("src"), lax.axis_index("dp")
    turn = count // 2
    places = [row // 2 % turn if row % 2 == 0 else count - 1 - row // 2 % turn for row in range(devices)]
    inward = [
        (row * count + part, (row // 2 // turn * count + part) * count + places[row])
        for row in range(devices)
        for part in range(count)
    ]
    outward = [(there, here) for here, there in inward]

    def enter(a):
        return lax.ppermute(a, ("dp", "src"), inward)

    def leave(a):
        return lax.ppermute(a, ("dp", "src"), outward)

    def spread(arrays, offsets, bit):
        came = []
        for array, offset in zip(arrays, offsets):
            pairs = [
                ((row ^ offset) * count + there, (row ^ offset ^ bit) * count + there)
                for row, there in enumerate(places)
            ]
            came.append(lax.ppermute(array, ("dp", "src"), pairs))
        return came

    def holder():
        return sum(
            number * ((me == there) & (me_dp == row ^ offset))
            for row, there in enumerate(places)
            for number, offset in enumerate(spread_order(count))
        )

    first = me * own
    ids = jnp.concatenate([src_ids.reshape(count, own), tgt_ids.reshape(count, own)], axis=0)
    ids = jnp.pad(ids, ((0, ID_ROWS - 2 * count), (0, features - own))).astype(BF)
    source = enter(src_tok[0])
    ids, target = lax.optimization_barrier((ids, tgt_tok[0]))
    names = enter(ids)
    source_first = exchange(source, count // 2, devices)
    names, source_first = lax.optimization_barrier((names, source_first))
    source_pieces = gather_rest(source, [source_first], count, devices)
    own_grad, source_pieces[-1] = lax.optimization_barrier((out_grad[0], source_pieces[-1]))
    own_grad = lax.dynamic_slice_in_dim(own_grad, first, own, 0)
    spreading, offsets, bit = [target], [0], count // 2
    spreading += spread(spreading, offsets, bit)
    which = holder()
    place = jnp.stack([lax.rem(me_dp, count), me_dp, which]).astype(jnp.int32)
    many = len(source_pieces)
    narrow, half = (own, features), (length // 2, features)
    shard = features // devices
    column = ((own, 1), F32)
    pair_stats = ((pairs, 2, own), F32)
    all_keys = ((length, 2 * features), BF)
    id_scratch = ((ID_ROWS, features), F32)
    bias_scratch = ((length, own), F32)
    small_product = ((devices, shard, features), BF)
    product = ((devices, hidden // devices, features), BF)

    def bucket(rows):
        return [((devices // 2, rows, features), BF)] * 2

    ffn_rows = 2 * shard * (hidden // features)

    order = Order(place)
    norm_columns = features + PAIR

    q_e, kv_e, stats_e, mixed_e, norms_e, memory = order.call(
        encoder_forward, many,
        [*map(Far, source_pieces), names, Far(enc_attn_in), Far(enc_attn_out), Far(enc_ffn_in), Far(enc_ffn_out), Far(enc_gains), Far(enc_biases)],
        [(narrow, BF, "far"), (*all_keys, "far"), (*pair_stats, "far"), (narrow, F32, "far"),
         ((own, 2 * norm_columns), F32, "far"), (narrow, BF)],
        [bias_scratch, id_scratch],
        11,
    )
    memory, spreading[-1] = lax.optimization_barrier((memory, spreading[-1]))
    memory_pieces = gather_near(memory, count, devices)
    offsets, bit = spread_order(count)[: len(spreading)], bit // 2
    while bit:
        spreading += spread(spreading, offsets, bit)
        offsets, bit = spread_order(count)[: len(spreading)], bit // 2
    target = Choice([a.reshape(count, own, features) for a in spreading])
    own_grad = enter(own_grad)
    q_d, kv_d, stats_d, mixed_d, norms_d = order.call(
        decoder_self_forward, many,
        [target, names, Far(dec_self_in), Far(dec_self_out)],
        [(narrow, BF, "far"), (*all_keys, "far"), (*pair_stats, "far"), (narrow, F32, "far"),
         ((own, norm_columns), F32)],
        [bias_scratch, id_scratch],
        9,
    )
    early_rows = ffn_rows + 4 * shard
    shards, out_own, memory_keep, memory_send, d_target, vectors_d = order.call(
        decoder_middle, many,
        [*memory_pieces, names, norms_d, own_grad, Far(dec_cross_q), Far(dec_cross_kv),
         Far(dec_cross_out), Far(dec_ffn_in), Far(dec_ffn_out), Far(dec_gains), Far(dec_biases)],
        [((devices, early_rows, features), BF, "far"), (narrow, BF, "far"), (half, BF), (half, BF),
         (narrow, F32), ((6, features), F32, "far")],
        [bias_scratch, id_scratch, (narrow, BF), all_keys, pair_stats, (narrow, F32), (narrow, BF),
         (narrow, BF), all_keys, ((length, features), BF)],
        28,
    )
    early = lax.psum_scatter(shards, "dp", scatter_dimension=0, tiled=True)[0]
    memory_sum = GroupSum(memory_keep, memory_send, count, devices)
    memory_sum.send()
    memory_sum.finish(order)
    target_keep, target_send, pack_d, dkv_d = order.call(
        decoder_self_back, many,
        [d_target, names, Far(q_d), Far(kv_d), Far(stats_d), Far(mixed_d), Far(dec_self_in),
         Far(dec_self_out)],
        [(half, BF), (half, BF), ((3 * own, features), BF, "far"), (*all_keys, "far")],
        [bias_scratch, id_scratch, (narrow, BF), (narrow, BF)],
        14,
    )
    target_sum = GroupSum(target_keep, target_send, count, devices)
    target_sum.send()
    d_source, vectors_e, send_u, keep_u = order.call(
        encoder_ffn_back, len(memory_sum.arrays),
        [*memory_sum.arrays, Far(norms_e), Far(enc_ffn_in), Far(enc_ffn_out), Far(enc_gains),
         Far(enc_biases)],
        [(narrow, F32), ((4, features), F32, "far"), *bucket(ffn_rows)],
        [product],
        9,
    )
    latter = DpSum(send_u, keep_u, devices)
    latter.step()
    target_sum.finish(order)
    source_keep, source_send, pack_e, dkv_e = order.call(
        encoder_attention_back, many,
        [d_source, names, Far(q_e), Far(kv_e), Far(stats_e), Far(mixed_e), Far(enc_attn_in),
         Far(enc_attn_out)],
        [(half, BF), (half, BF), ((3 * own, features), BF, "far"), (*all_keys, "far")],
        [bias_scratch, id_scratch, (narrow, BF), (narrow, BF)],
        14,
    )
    source_sum = GroupSum(source_keep, source_send, count, devices)
    source_sum.send()
    send_s, keep_s = order.call(
        late_weights, many,
        [*map(Far, source_pieces), target,
         *map(Far, [pack_d, dkv_d, pack_e, dkv_e, vectors_d, vectors_e])],
        bucket(8 * shard + VECTOR_ROWS),
        [small_product, ((length, features), BF)],
        6, [*target_sum.arrays[1:], *latter.parts],
    )
    back = leave(jnp.stack([out_own, first_rows(target_sum.arrays, own).astype(BF)]))
    former = DpSum(send_s, keep_s, devices)
    former.step()
    latter.step()
    early, back, source_sum.arrays, former.parts, latter.parts = fence(
        early, back, source_sum.arrays, former.parts, latter.parts
    )
    early = LineSum(early, count)
    early.step()
    back = lax.all_gather(back, "src", axis=1, tiled=True)
    dec_out, tgt_grad = back[0], back[1]
    while not source_sum.done():
        rows = source_sum.arrays[-1].shape[0] // 2
        source_sum.to_send = first_rows([a[rows:] for a in source_sum.arrays], rows).astype(BF)
        source_sum.send()
    former.step()
    while latter.left:
        latter.step()
    src_grad = leave(first_rows(source_sum.arrays, own).astype(BF))
    early.parts, src_grad, former.parts, latter.parts = fence(
        early.parts, src_grad, former.parts, latter.parts
    )
    early.step()
    latter = LineSum(jnp.concatenate(latter.parts, axis=0), count)
    latter.step()
    while former.left:
        former.step()
    early.parts, latter.parts, former.parts = fence(early.parts, latter.parts, former.parts)
    lines = [LineSum(jnp.concatenate(former.parts, axis=0), count), latter, early]
    while any(line.hop < count - 1 for line in lines):
        for line in lines:
            if line.hop < count - 1:
                line.step()
    selfs, ffn_e, early = (line.parts[0].astype(F32) for line in lines)
    src_grad = src_grad.astype(F32)
    tgt_grad = tgt_grad.astype(F32)
    self_d, attn_e = selfs[: 4 * shard], selfs[4 * shard :]
    ffn_d, cross = early[:ffn_rows], early[ffn_rows:]

    def wide(rows):
        return jnp.concatenate(jnp.split(rows, rows.shape[0] // shard, axis=0), axis=1)

    up = shard * (hidden // features)
    vectors = attn_e[4 * shard :]
    vectors = lax.dynamic_slice_in_dim(vectors, me_dp * shard, shard, 1)
    return (
        dec_out[None],
        src_grad[None],
        tgt_grad[None],
        wide(attn_e[: 3 * shard]),
        attn_e[3 * shard : 4 * shard],
        wide(ffn_e[:up]),
        ffn_e[up:],
        jnp.stack([vectors[8], vectors[6]]),
        jnp.stack([vectors[9], vectors[7]]),
        wide(self_d[: 3 * shard]),
        self_d[3 * shard :],
        cross[shard : 2 * shard],
        wide(cross[2 * shard :]),
        cross[:shard],
        wide(ffn_d[:up]),
        ffn_d[up:],
        jnp.stack([vectors[4], vectors[2], vectors[0]]),
        jnp.stack([vectors[5], vectors[3], vectors[1]]),
    )


def solution(mesh):
    row, part = P("dp", None, None), P("dp", "src", None)
    line, rows, columns = P("dp", None), P("dp", None), P(None, "dp")
    in_specs = (part, line, row, line, row) + (P(),) * 15
    out_specs = (
        row, part, row, rows, rows, rows, rows, columns, columns,
        rows, rows, rows, rows, rows, rows, rows, columns, columns,
    )
    return jax.shard_map(local, mesh=mesh, in_specs=in_specs, out_specs=out_specs, check_vma=False)
```

```python
import functools
import math

import jax
import jax.numpy as jnp
from jax import lax
from jax.experimental import pallas as pl
from jax.experimental.pallas import tpu as pltpu
from jax.sharding import PartitionSpec as P

HEAD_DIM = 64
PAIR = 2 * HEAD_DIM
EPS = 1e-05
NEGATIVE = -1e30
BF = jnp.bfloat16
F32 = jnp.float32
BLOCK = 1024
VECTOR_ROWS = 32
ID_ROWS = 16
LIMIT = 34


def dot(former, latter, dims):
    return lax.dot_general(former, latter, (dims, ((), ())), preferred_element_type=F32)


def nn(former, latter):
    return dot(former, latter, ((1,), (0,)))


def nt(former, latter):
    return dot(former, latter, ((1,), (1,)))


def tn(former, latter):
    return dot(former, latter, ((0,), (0,)))


def norm(v):
    centred = v - jnp.mean(v, axis=-1, keepdims=True)
    inverse = lax.rsqrt(jnp.mean(centred * centred, axis=-1, keepdims=True) + EPS)
    return centred * inverse, inverse


def norm_back(du, normed, inverse, gain):
    gain_grad = jnp.sum(du * normed, axis=0, keepdims=True)
    bias_grad = jnp.sum(du, axis=0, keepdims=True)
    scaled = du * gain
    mean = jnp.mean(scaled, axis=-1, keepdims=True)
    slope = jnp.mean(scaled * normed, axis=-1, keepdims=True)
    return inverse * (scaled - mean - normed * slope), gain_grad, bias_grad


def head_halves(pair, scale):
    wide = pair.astype(F32) * scale
    first = lax.broadcasted_iota(jnp.int32, wide.shape, 1) < HEAD_DIM
    return [jnp.where(first, wide, 0.0).astype(BF), jnp.where(first, 0.0, wide).astype(BF)]


def pair_columns(pair, offset=0):
    return pl.ds(pl.multiple_of(pair * PAIR + offset, PAIR), PAIR)


def mask_bias(key_ids, query_ids):
    return jnp.where(key_ids == query_ids, 0.0, NEGATIVE)


def pair_forward(q, k, v, bias):
    queries = head_halves(q, HEAD_DIM**-0.5)
    values = v.T
    mixed, stats = [], []
    for head in range(2):
        s = nt(k, queries[head]) + bias
        maximum = jnp.max(s, axis=0, keepdims=True)
        e = jnp.exp(s - maximum)
        total = jnp.sum(e, axis=0, keepdims=True)
        o = nn(values[head * HEAD_DIM : (head + 1) * HEAD_DIM], e.astype(BF))
        mixed.append(o * (1.0 / total))
        stats.append(maximum + jnp.log(total))
    return jnp.concatenate(mixed, axis=0).T, jnp.concatenate(stats, axis=0)


def pair_delta(o, grad):
    product = (o * grad.astype(F32)).T
    return (
        jnp.sum(product[:HEAD_DIM], axis=0, keepdims=True),
        jnp.sum(product[HEAD_DIM:], axis=0, keepdims=True),
    )


def block_backward(qs, gs, k, v, keys, bias, stats, deltas):
    dq, dk, dv = [], None, None
    for head in range(2):
        s = nt(k, qs[head]) + bias
        p = jnp.exp(s - stats[head : head + 1])
        ds = (p * (nt(v, gs[head]) - deltas[head])).astype(BF)
        p = p.astype(BF)
        dq.append(nn(keys[head * HEAD_DIM : (head + 1) * HEAD_DIM], ds))
        dk_term, dv_term = nn(ds, qs[head]), nn(p, gs[head])
        dk = dk_term if dk is None else dk + dk_term
        dv = dv_term if dv is None else dv + dv_term
    return jnp.concatenate(dq, axis=0), dk, dv


def cross_backward(q_ref, kv_ref, o_ref, g_ref, bias_ref, stats_ref, dq_ref, dkv_ref):
    features = q_ref.shape[1]
    keys_count = kv_ref.shape[0]

    def one_pair(pair, carry):
        columns = pair_columns(pair)
        value_columns = pair_columns(pair, features)
        q, g = q_ref[:, columns], g_ref[:, columns]
        qs = head_halves(q, HEAD_DIM**-0.5)
        gs = head_halves(g, 1.0)
        deltas = pair_delta(o_ref[:, columns], g)
        stats = stats_ref[pair]
        total = None
        for first in range(0, keys_count, BLOCK):
            rows = slice(first, first + BLOCK)
            k = kv_ref[rows, columns]
            term, dk, dv = block_backward(
                qs, gs, k, kv_ref[rows, value_columns], k.T, bias_ref[rows, :], stats, deltas
            )
            dkv_ref[rows, columns] = dk.astype(BF)
            dkv_ref[rows, value_columns] = dv.astype(BF)
            total = term if total is None else total + term
        dq_ref[:, columns] = (total.T * HEAD_DIM**-0.5).astype(BF)
        return carry

    lax.fori_loop(0, features // PAIR, one_pair, 0)


def emit(me_dp, product, former, latter, send, keep, offset):
    devices = 2 * send.shape[0]
    width = product.shape[2]
    height = former.shape[1]
    rows = height // devices
    for first in range(0, latter.shape[1], width):
        term = tn(former, latter[:, first : first + width]).astype(BF)
        product[:, :rows, :] = term.reshape(devices, rows, width)
        for slot in range(devices):
            target = send if slot % 2 else keep
            target[slot // 2, offset : offset + rows, :] = product[
                jnp.bitwise_xor(me_dp, slot), :rows, :
            ]
        offset += rows
    return offset


def sigmoid(v):
    return 1.0 / (1.0 + jnp.exp(-v))


def silu_parts(pre):
    squashed = sigmoid(pre)
    return pre * squashed, squashed * (1.0 + pre * (1.0 - squashed))


def near_order(count):
    order, bit = [0], 1
    while bit < count:
        order += [o ^ bit for o in order]
        bit *= 2
    return order


def near_blocks(refs, own, count):
    found = blocks_of(refs, own, own)
    return [found[near_order(count).index(o)] for o in key_order(count)]


def blocks_of(refs, height, own):
    found = []
    for ref in refs:
        for first in range(0, ref.shape[0], height):
            found.append((ref, slice(first, first + own)))
    return found


def key_order(count):
    order = [0]
    bit = count // 2
    while bit:
        order += [o ^ bit for o in order]
        bit //= 2
    return order


def spread_order(count):
    order, bit = [0], count // 2
    while bit:
        order += [o ^ bit for o in order]
        bit //= 2
    return order


def fill_bias(bias, ids, first_key, first_query, member, causal):
    keys_count, own = bias.shape
    count = keys_count // own
    lines = ids[:, :own]
    numbers = lax.broadcasted_iota(jnp.int32, lines.shape, 0)

    def pick(row):
        return jnp.sum(jnp.where(numbers == row, lines, 0.0), axis=0, keepdims=True)

    queries = pick(first_query + member)
    for number, offset in enumerate(key_order(count)):
        peer = jnp.bitwise_xor(member, offset)
        line = jnp.broadcast_to(pick(first_key + peer), (128, own)).T
        line = jnp.concatenate([line] * (own // 128), axis=1)
        term = mask_bias(line, queries)
        if causal:
            keys = lax.broadcasted_iota(jnp.int32, term.shape, 0) + (peer - member) * own
            term = jnp.where(keys <= lax.broadcasted_iota(jnp.int32, term.shape, 1), term, NEGATIVE)
        bias[number * own : (number + 1) * own, :] = term


def attend(q, kv, bias, mixed, stats):
    features = q.shape[1]

    def one_pair(pair, carry):
        columns = pair_columns(pair)
        o, logsum = pair_forward(
            q[:, columns], kv[:, columns], kv[:, pair_columns(pair, features)], bias[...]
        )
        mixed[:, columns] = o
        stats[pair] = logsum
        return carry

    lax.fori_loop(0, features // PAIR, one_pair, 0)


def project(blocks, weight, columns, target):
    for number, (ref, rows) in enumerate(blocks):
        own = rows.stop - rows.start
        target[number * own : (number + 1) * own, :] = nn(ref[rows, :], weight[:, columns]).astype(BF)


def put_norm(target, number, normed, inverse):
    features = normed.shape[1]
    count = target.shape[1] // (features + PAIR)
    target[:, number * features : (number + 1) * features] = normed
    first = count * features + number * PAIR
    target[:, first : first + PAIR] = jnp.broadcast_to(inverse, (inverse.shape[0], PAIR))


def get_norm(source, number, features):
    count = source.shape[1] // (features + PAIR)
    first = count * features + number * PAIR
    return source[:, number * features : (number + 1) * features], source[:, first : first + 1]


def encoder_forward(io, many, refs):
    pieces = refs[:many]
    (names, w_in, w_out, w_up, w_down, gains, biases,
     q, kv, stats, mixed, norms, memory, bias, ids) = refs[many:]
    own, features = q.shape
    blocks = blocks_of(pieces, own, own)
    io.ready(pieces[0], w_in)
    q[...] = nn(pieces[0][...], w_in[:, :features]).astype(BF)
    io.ready(*pieces)
    project(blocks, w_in, slice(features, 3 * features), kv)
    ids[...] = names[...].astype(F32)
    fill_bias(bias, ids, 0, 0, io.place[0], False)
    attend(q, kv, bias, mixed, stats)
    io.flush(q, kv, stats, mixed)
    io.ready(w_out, gains, biases, w_up, w_down)
    v = pieces[0][...].astype(F32) + nn(mixed[...].astype(BF), w_out[...])
    normed, inverse = norm(v)
    put_norm(norms, 0, normed, inverse)
    x1 = normed * gains[0:1, :] + biases[0:1, :]
    pre = nn(x1.astype(BF), w_up[...])
    hidden = (pre * sigmoid(pre)).astype(BF)
    normed, inverse = norm(x1 + nn(hidden, w_down[...]))
    put_norm(norms, 1, normed, inverse)
    memory[...] = (normed * gains[1:2, :] + biases[1:2, :]).astype(BF)


def decoder_self_forward(io, many, refs):
    tokens, names, w_in, w_out, q, kv, stats, mixed, norms, bias, ids = refs
    own, features = q.shape
    count = tokens.shape[0]
    member = io.place[0]
    io.ready(names, tokens, w_in)
    ids[...] = names[...].astype(F32)
    mine = tokens[member]
    q[...] = nn(mine, w_in[:, :features]).astype(BF)
    for number, offset in enumerate(key_order(count)):
        kv[number * own : (number + 1) * own, :] = nn(
            tokens[jnp.bitwise_xor(member, offset)], w_in[:, features:]
        ).astype(BF)
    fill_bias(bias, ids, count, count, member, True)
    attend(q, kv, bias, mixed, stats)
    io.flush(q, kv, stats, mixed)
    io.ready(w_out)
    normed, inverse = norm(mine.astype(F32) + nn(mixed[...].astype(BF), w_out[...]))
    put_norm(norms, 0, normed, inverse)


def decoder_middle(io, many, refs):
    pieces = refs[:many]
    (names, norms, out_grad, w_q, w_kv, w_out, w_up, w_down, gains, biases,
     shards, dec_out, memory_keep, memory_send, d_target, vectors,
     bias, ids, q, kv, stats, mixed, dq, grad, dkv, memory) = refs[many:]
    own, features = q.shape
    count = kv.shape[0] // own
    half = memory_keep.shape[0]
    io.ready(names, norms, gains, biases, w_q)
    ids[...] = names[...].astype(F32)
    normed_c, inverse_c = get_norm(norms, 0, features)
    y1 = normed_c * gains[0:1, :] + biases[0:1, :]
    y1_low = y1.astype(BF)
    q[...] = nn(y1_low, w_q[...]).astype(BF)
    io.ready(w_kv, *pieces)
    project(near_blocks(pieces, own, count), w_kv, slice(None), kv)
    fill_bias(bias, ids, 0, count, io.place[0], False)
    attend(q, kv, bias, mixed, stats)
    io.ready(w_out, w_up, w_down, out_grad)
    mixed_low = mixed[...].astype(BF)
    normed_d, inverse_d = norm(y1 + nn(mixed_low, w_out[...]))
    y2 = normed_d * gains[1:2, :] + biases[1:2, :]
    y2_low = y2.astype(BF)
    act, slope = silu_parts(nn(y2_low, w_up[...]))
    hidden = act.astype(BF)
    normed, inverse = norm(y2 + nn(hidden, w_down[...]))
    dec_out[...] = (normed * gains[2:3, :] + biases[2:3, :]).astype(BF)
    dv, gain_grad, bias_grad = norm_back(
        out_grad[...].astype(F32), normed, inverse, gains[2:3, :]
    )
    vectors[0:1, :] = gain_grad
    vectors[1:2, :] = bias_grad
    dv_low = dv.astype(BF)
    d_pre = (nt(dv_low, w_down[...]) * slope).astype(BF)
    devices, _, width = shards.shape
    offset = 0

    def emit_all(former, latter, offset):
        rows = former.shape[1] // devices
        for first in range(0, latter.shape[1], width):
            term = tn(former, latter[:, first : first + width]).astype(BF)
            shards[:, offset : offset + rows, :] = term.reshape(devices, rows, width)
            offset += rows
        return offset

    offset = emit_all(y2_low, d_pre, offset)
    offset = emit_all(hidden, dv_low, offset)
    io.flush(dec_out)
    d_second = dv + nt(d_pre, w_up[...])
    dv, gain_grad, bias_grad = norm_back(d_second, normed_d, inverse_d, gains[1:2, :])
    vectors[2:3, :] = gain_grad
    vectors[3:4, :] = bias_grad
    dv_low = dv.astype(BF)
    offset = emit_all(mixed_low, dv_low, offset)
    grad[...] = nt(dv_low, w_out[...]).astype(BF)
    cross_backward(q, kv, mixed, grad, bias, stats, dq, dkv)
    offset = emit_all(y1_low, dq[...], offset)
    emit_all(whole(near_blocks(pieces, own, count), memory), dkv[...], offset)
    io.flush(shards)
    memory_send[...] = nt(dkv[half:, :], w_kv[...]).astype(BF)
    memory_keep[...] = nt(dkv[:half, :], w_kv[...]).astype(BF)
    io.flush(memory_send, memory_keep)
    d_first = dv + nt(dq[...], w_q[...])
    dv, gain_grad, bias_grad = norm_back(d_first, normed_c, inverse_c, gains[0:1, :])
    vectors[4:5, :] = gain_grad
    vectors[5:6, :] = bias_grad
    d_target[...] = dv


def whole(blocks, target):
    for number, (ref, rows) in enumerate(blocks):
        own = rows.stop - rows.start
        target[number * own : (number + 1) * own, :] = ref[rows, :]
    return target[...]


def self_back(io, refs, first_id, causal):
    (dv, names, q, kv, stats, mixed, w_in, w_out, keep, send, pack, dkv, bias, ids, grad, dq) = refs
    own, features = q.shape
    half = keep.shape[0]
    io.ready(names, dv, mixed, w_out)
    ids[...] = names[...].astype(F32)
    fill_bias(bias, ids, first_id, first_id, io.place[0], causal)
    dv_low = dv[...].astype(BF)
    pack[own : 2 * own, :] = dv_low
    pack[2 * own :, :] = mixed[...].astype(BF)
    grad[...] = nt(dv_low, w_out[...]).astype(BF)
    io.ready(q, kv, stats)
    cross_backward(q, kv, mixed, grad, bias, stats, dq, dkv)
    pack[:own, :] = dq[...]
    io.flush(pack, dkv)
    io.ready(w_in)
    send[...] = nt(dkv[half:, :], w_in[:, features:]).astype(BF)
    io.flush(send)
    term = nt(dkv[:half, :], w_in[:, features:])
    keep[own:, :] = term[own:].astype(BF)
    keep[:own, :] = (term[:own] + dv[...] + nt(dq[...], w_in[:, :features])).astype(BF)


def decoder_self_back(io, many, refs):
    q, kv = refs[2:4]
    self_back(io, refs, kv.shape[0] // q.shape[0], True)


def encoder_attention_back(io, many, refs):
    self_back(io, refs, 0, False)


def emit_self(io, tokens, pack, dkv, send, keep, product, offset):
    own = pack.shape[0] // 3
    offset = emit(io.place[1], product, tokens[:own, :], pack[:own, :], send, keep, offset)
    offset = emit(io.place[1], product, tokens[...], dkv[...], send, keep, offset)
    return emit(
        io.place[1], product, pack[2 * own :, :], pack[own : 2 * own, :], send, keep, offset
    )


def encoder_ffn_back(io, many, refs):
    d_memory = refs[:many]
    norms, w_up, w_down, gains, biases, d_source, vectors, send, keep, product = refs[many:]
    own, features = d_source.shape
    io.ready(*d_memory, norms, gains, biases)
    du = first_rows(d_memory, own)
    dv, gain_grad, bias_grad = norm_back(du, *get_norm(norms, 1, features), gains[1:2, :])
    vectors[0:1, :] = gain_grad
    vectors[1:2, :] = bias_grad
    dv_low = dv.astype(BF)
    normed_a, inverse_a = get_norm(norms, 0, features)
    x1_low = (normed_a * gains[0:1, :] + biases[0:1, :]).astype(BF)
    io.ready(w_up, w_down)
    act, slope = silu_parts(nn(x1_low, w_up[...]))
    hidden = act.astype(BF)
    d_pre = (nt(dv_low, w_down[...]) * slope).astype(BF)
    offset = emit(io.place[1], product, x1_low, d_pre, send, keep, 0)
    emit(io.place[1], product, hidden, dv_low, send, keep, offset)
    d_mid = dv + nt(d_pre, w_up[...])
    dv, gain_grad, bias_grad = norm_back(d_mid, normed_a, inverse_a, gains[0:1, :])
    vectors[2:3, :] = gain_grad
    vectors[3:4, :] = bias_grad
    d_source[...] = dv


def late_weights(io, many, refs):
    pieces = refs[:many]
    (tokens, pack_d, dkv_d, pack_e, dkv_e, vectors_d, vectors_e,
     send, keep, product, ordered) = refs[many:]
    count, own, features = tokens.shape
    io.ready(tokens, pack_d, dkv_d)
    for number, peer in enumerate(key_order(count)):
        rows = slice(number * own, (number + 1) * own)
        ordered[rows, :] = tokens[jnp.bitwise_xor(io.place[0], peer)]
    offset = emit_self(io, ordered, pack_d, dkv_d, send, keep, product, 0)
    io.ready(*pieces, pack_e, dkv_e, vectors_d, vectors_e)
    whole(blocks_of(pieces, own, own), ordered)
    offset = emit_self(io, ordered, pack_e, dkv_e, send, keep, product, offset)
    rows = jnp.concatenate(
        [vectors_d[...], vectors_e[...], jnp.zeros((VECTOR_ROWS - 10, features), F32)], axis=0
    ).astype(BF)
    for slot in range(send.shape[0]):
        send[slot, offset : offset + VECTOR_ROWS, :] = rows
        keep[slot, offset : offset + VECTOR_ROWS, :] = rows


class Far:
    def __init__(self, array):
        self.array = array


class Choice:
    def __init__(self, arrays):
        self.arrays = arrays


class ChosenCopy:
    def __init__(self, place, sources, target, semaphore):
        self.which = place[2]
        self.copies = [pltpu.make_async_copy(a, target, semaphore) for a in sources]

    def start(self):
        for number, copy in enumerate(self.copies):
            pl.when(self.which == number)(copy.start)

    def wait(self):
        self.copies[0].wait()


class Io:
    def __init__(self, place, arriving, leaving):
        self.place, self.arriving, self.leaving, self.gone = place, arriving, leaving, []
        for copy in arriving.values():
            copy.start()

    def ready(self, *refs):
        for ref in refs:
            copy = self.arriving.pop(id(ref), None)
            if copy is not None:
                copy.wait()

    def flush(self, *refs):
        for ref in refs:
            copy = self.leaving.pop(id(ref), None)
            if copy is not None:
                copy.start()
                self.gone.append(copy)

    def finish(self):
        for copy in self.arriving.values():
            copy.wait()
        for copy in self.leaving.values():
            copy.start()
        for copy in [*self.gone, *self.leaving.values()]:
            copy.wait()


class Order:
    def __init__(self, place):
        self.place = place

    def run(self, body, name, operands, outs, in_specs, out_specs, scratch, weight, grid=()):
        moved = sum(math.prod(a.shape) * a.dtype.itemsize for a in (*operands, *outs))
        found = pl.pallas_call(
            body,
            name=name,
            grid=grid,
            out_shape=[jax.ShapeDtypeStruct((3,), jnp.int32), *outs],
            in_specs=[pl.BlockSpec(memory_space=pltpu.SMEM), *in_specs],
            out_specs=[pl.BlockSpec(memory_space=pltpu.SMEM), *out_specs],
            scratch_shapes=scratch,
            compiler_params=pltpu.CompilerParams(vmem_limit_bytes=LIMIT * 1024 * 1024),
            cost_estimate=pl.CostEstimate(
                flops=int(weight * 1.15e9), bytes_accessed=int(moved), transcendentals=0
            ),
        )(self.place, *operands)
        self.place = found[0]
        return list(found[1:])

    def call(self, kernel, many, operands, outs, scratch, weight, ties=()):
        far_out = [i for i, out in enumerate(outs) if len(out) == 3]
        groups, flat, spaces, held = [], [], [], []
        for a in operands:
            if isinstance(a, (Far, Choice)):
                arrays = a.arrays if isinstance(a, Choice) else [a.array]
                held.append(arrays[0])
                arrays = [pltpu.with_memory_space_constraint(one, pltpu.HBM) for one in arrays]
                space = pltpu.HBM
            else:
                arrays, space = [a], pltpu.VMEM
            groups.append((slice(len(flat), len(flat) + len(arrays)), space == pltpu.HBM))
            flat += arrays
            spaces += [pl.BlockSpec(memory_space=space)] * len(arrays)
        outs = [jax.ShapeDtypeStruct(*out[:2]) for out in outs]
        count, tied, far_in = len(flat), len(ties), len(held)

        def wrapped(place, *refs):
            sources, refs = refs[:count], refs[count + tied :]
            after, results, refs = refs[0], list(refs[1 : 1 + len(outs)]), refs[1 + len(outs) :]
            here, refs = list(refs[:far_in]), refs[far_in:]
            inputs, arriving, leaving = [], {}, {}
            for places, far in groups:
                if far:
                    target = here[len(arriving)]
                    semaphore = refs[-2].at[len(arriving)]
                    arriving[id(target)] = ChosenCopy(place, sources[places], target, semaphore)
                    if places.stop - places.start == 1:
                        arriving[id(target)] = arriving[id(target)].copies[0]
                    inputs.append(target)
                else:
                    inputs.append(sources[places.start])
            for number, i in enumerate(far_out):
                target = refs[number]
                leaving[id(target)] = pltpu.make_async_copy(target, results[i], refs[-1].at[number])
                results[i] = target
            refs = refs[len(far_out) : -2]
            for i in range(3):
                after[i] = place[i]
            io = Io(place, arriving, leaving)
            kernel(io, many, (*inputs, *results, *refs))
            io.finish()

        held += [outs[i] for i in far_out]
        out_specs = [
            pl.BlockSpec(memory_space=pltpu.HBM if i in far_out else pltpu.VMEM)
            for i in range(len(outs))
        ]
        outs = [pltpu.HBM(a.shape, a.dtype) if i in far_out else a for i, a in enumerate(outs)]
        return self.run(
            wrapped, kernel.__name__, [*flat, *ties], outs,
            spaces + [pl.BlockSpec(memory_space=pl.ANY)] * tied, out_specs,
            [pltpu.VMEM(a.shape, a.dtype) for a in held]
            + [pltpu.VMEM(shape, dtype) for shape, dtype in scratch]
            + [pltpu.SemaphoreType.DMA((max(1, n),)) for n in (far_in, len(far_out))],
            weight,
        )

    def batch(self, tasks, weight, ties=()):
        operands = [a for task in tasks for a in task[1]]
        outs = [out for task in tasks for out in task[2]]

        def batch(io, many, refs):
            inputs, results = list(refs[: len(operands)]), list(refs[len(operands) :])
            for kernel, taken, given in tasks:
                kernel(io, 0, (*inputs[: len(taken)], *results[: len(given)]))
                del inputs[: len(taken)], results[: len(given)]

        found = self.call(batch, 0, operands, outs, [], weight, ties)
        return [[found.pop(0) for _ in task[2]] for task in tasks]


def first_rows(parts, own):
    return functools.reduce(lambda a, b: a + b, [part[:own, :].astype(F32) for part in parts])


def group_last(io, many, refs):
    *parts, total = refs
    total[...] = first_rows(parts, total.shape[0]).astype(BF)


def add_rows(io, many, refs):
    *parts, total = refs
    rows = slice(total.shape[0], 2 * total.shape[0])
    total[...] = functools.reduce(
        lambda a, b: a + b, [part[rows, :].astype(F32) for part in parts]
    ).astype(BF)


def add_line(io, many, refs):
    own, came, carried = refs
    carried[...] = (own[...].astype(F32) + came[...].astype(F32)).astype(BF)


def exchange(part, bit, devices):
    return lax.ppermute(part, "dp", [(i, i ^ bit) for i in range(devices)])


def gather_group(own, count, devices):
    arrays, held, bit = [own], own, count // 2
    while bit:
        arrays.append(exchange(held, bit, devices))
        if bit > 1:
            held = jnp.concatenate([held, arrays[-1]], axis=0)
        bit //= 2
    return arrays


def gather_near(own, count, devices):
    arrays, bit = [own], 1
    while bit < count:
        held = jnp.concatenate(arrays, axis=0) if bit > 1 else own
        arrays.append(exchange(held, bit, devices))
        bit *= 2
    return arrays


def gather_rest(own, first, count, devices):
    arrays, bit = [own, *first], count // 4
    while bit:
        held = jnp.concatenate(arrays, axis=0)
        arrays.append(exchange(held, bit, devices))
        bit //= 2
    return arrays


class GroupSum:
    def __init__(self, keep, send, count, devices):
        self.arrays, self.to_send, self.bit = [keep], send, 1
        self.count, self.devices = count, devices

    def send(self):
        self.arrays.append(exchange(self.to_send, self.bit, self.devices))
        self.bit *= 2

    def done(self):
        return self.bit >= self.count

    def task(self):
        rows, columns = self.arrays[-1].shape
        return add_rows, self.arrays, [((rows // 2, columns), BF)]

    def take(self, found):
        (self.to_send,) = found

    def finish(self, order):
        while not self.done():
            self.take(*order.batch([self.task()], 1))
            self.send()


def add_parts(io, many, refs):
    kept_a, came_a, kept_b, came_b, send_a, keep_a, send_b, keep_b = refs
    cut, half = keep_a.shape[1], keep_a.shape[0]
    first = kept_b.shape[1] - keep_b.shape[1]

    def total(kept, came, index, rows):
        return (kept[index, rows, :].astype(F32) + came[index, rows, :].astype(F32)).astype(BF)

    for number in range(half):
        send_a[number] = total(kept_a, came_a, 2 * number + 1, slice(0, cut))
        keep_a[number] = total(kept_a, came_a, 2 * number, slice(0, cut))
        send_b[number] = total(kept_b, came_b, half + number, slice(first, None))
        keep_b[number] = total(kept_b, came_b, number, slice(first, None))


def add_last(io, many, refs):
    kept_a, came_a, kept_b, came_b, total = refs
    cut = kept_a.shape[1]
    total[:cut, :] = (kept_a[0].astype(F32) + came_a[0].astype(F32)).astype(BF)
    total[cut:, :] = (kept_b[0].astype(F32) + came_b[0].astype(F32)).astype(BF)


def add_two(io, many, refs):
    kept_a, came_a, kept_b, came_b, first, second = refs
    first[...] = (kept_a[0].astype(F32) + came_a[0].astype(F32)).astype(BF)
    second[...] = (kept_b[0].astype(F32) + came_b[0].astype(F32)).astype(BF)


class DpSum:
    def __init__(self, send, keep, devices):
        self.send, self.parts, self.devices = send, [keep], devices
        self.left = list(range(devices.bit_length() - 2))

    def step(self):
        if self.send is not None:
            total = self.parts[0] + exchange(self.send, 1, self.devices)
            cut = total.shape[1] // 32 * 16
            self.parts, self.send = [total[:, :cut], total[:, cut:]], None
            self.orders = [self.left[:], self.left[::-1]]
            return
        found = []
        for part, order in zip(self.parts, self.orders):
            bit = order[0]
            part = part.reshape(-1, 2, 1 << sorted(order).index(bit), *part.shape[1:])
            part = part[:, 0] + exchange(part[:, 1], 2 << bit, self.devices)
            part = part.reshape(-1, *part.shape[2:])
            order.remove(bit)
            found.append(part if order else part[0])
        self.parts, self.left = found, self.orders[0]


def fence(*arrays):
    return lax.optimization_barrier(arrays)


class LineSum:
    def __init__(self, own, count):
        self.parts, self.count, self.hop = [own, own, own], count, 0

    def step(self):
        self.hop += 1
        hop, count = self.hop, self.count
        total, own, carried = self.parts
        pairs = [(hop - 1, hop), (count - hop, count - hop - 1)]
        came = lax.ppermute(carried, "src", pairs)
        self.parts = [total + came, own, own + came]


def local(
    src_tok, src_ids, tgt_tok, tgt_ids, out_grad,
    enc_attn_in, enc_attn_out, enc_ffn_in, enc_ffn_out, enc_gains, enc_biases,
    dec_self_in, dec_self_out, dec_cross_q, dec_cross_kv, dec_cross_out,
    dec_ffn_in, dec_ffn_out, dec_gains, dec_biases,
):
    count, devices = lax.axis_size("src"), lax.axis_size("dp")
    _, own, features = src_tok.shape
    length = tgt_tok.shape[1]
    pairs = features // PAIR
    hidden = enc_ffn_in.shape[1]
    me, me_dp = lax.axis_index("src"), lax.axis_index("dp")
    turn = count // 2
    places = [row // 2 % turn if row % 2 == 0 else count - 1 - row // 2 % turn for row in range(devices)]
    inward = [
        (row * count + part, (row // 2 // turn * count + part) * count + places[row])
        for row in range(devices)
        for part in range(count)
    ]
    outward = [(there, here) for here, there in inward]

    def enter(a):
        return lax.ppermute(a, ("dp", "src"), inward)

    def leave(a):
        return lax.ppermute(a, ("dp", "src"), outward)

    def spread(arrays, offsets, bit):
        came = []
        for array, offset in zip(arrays, offsets):
            pairs = [
                ((row ^ offset) * count + there, (row ^ offset ^ bit) * count + there)
                for row, there in enumerate(places)
            ]
            came.append(lax.ppermute(array, ("dp", "src"), pairs))
        return came

    def holder():
        return sum(
            number * ((me == there) & (me_dp == row ^ offset))
            for row, there in enumerate(places)
            for number, offset in enumerate(spread_order(count))
        )

    first = me * own
    ids = jnp.concatenate([src_ids.reshape(count, own), tgt_ids.reshape(count, own)], axis=0)
    ids = jnp.pad(ids, ((0, ID_ROWS - 2 * count), (0, features - own))).astype(BF)
    source = enter(src_tok[0])
    ids, target = lax.optimization_barrier((ids, tgt_tok[0]))
    names = enter(ids)
    source_first = exchange(source, count // 2, devices)
    names, source_first = lax.optimization_barrier((names, source_first))
    source_pieces = gather_rest(source, [source_first], count, devices)
    own_grad, names = lax.optimization_barrier((out_grad[0], names))
    own_grad = lax.dynamic_slice_in_dim(own_grad, first, own, 0)
    spreading, offsets, bit = [target], [0], count // 2
    spreading += spread(spreading, offsets, bit)
    which = holder()
    place = jnp.stack([lax.rem(me_dp, count), me_dp, which]).astype(jnp.int32)
    many = len(source_pieces)
    narrow, half = (own, features), (length // 2, features)
    shard = features // devices
    column = ((own, 1), F32)
    pair_stats = ((pairs, 2, own), F32)
    all_keys = ((length, 2 * features), BF)
    id_scratch = ((ID_ROWS, features), F32)
    bias_scratch = ((length, own), F32)
    small_product = ((devices, shard, features), BF)
    product = ((devices, hidden // devices, features), BF)

    def bucket(rows):
        return [((devices // 2, rows, features), BF)] * 2

    ffn_rows = 2 * shard * (hidden // features)

    order = Order(place)
    norm_columns = features + PAIR

    q_e, kv_e, stats_e, mixed_e, norms_e, memory = order.call(
        encoder_forward, many,
        [*map(Far, source_pieces), names, Far(enc_attn_in), Far(enc_attn_out), Far(enc_ffn_in), Far(enc_ffn_out), Far(enc_gains), Far(enc_biases)],
        [(narrow, BF, "far"), (*all_keys, "far"), (*pair_stats, "far"), (narrow, F32, "far"),
         ((own, 2 * norm_columns), F32, "far"), (narrow, BF)],
        [bias_scratch, id_scratch],
        11,
    )
    memory, spreading[-1] = lax.optimization_barrier((memory, spreading[-1]))
    memory_pieces = gather_near(memory, count, devices)
    offsets, bit = spread_order(count)[: len(spreading)], bit // 2
    while bit:
        spreading += spread(spreading, offsets, bit)
        offsets, bit = spread_order(count)[: len(spreading)], bit // 2
    target = Choice([a.reshape(count, own, features) for a in spreading])
    own_grad = enter(own_grad)
    q_d, kv_d, stats_d, mixed_d, norms_d = order.call(
        decoder_self_forward, many,
        [target, names, Far(dec_self_in), Far(dec_self_out)],
        [(narrow, BF, "far"), (*all_keys, "far"), (*pair_stats, "far"), (narrow, F32, "far"),
         ((own, norm_columns), F32)],
        [bias_scratch, id_scratch],
        9,
    )
    early_rows = ffn_rows + 4 * shard
    shards, out_own, memory_keep, memory_send, d_target, vectors_d = order.call(
        decoder_middle, many,
        [*memory_pieces, names, norms_d, own_grad, Far(dec_cross_q), Far(dec_cross_kv),
         Far(dec_cross_out), Far(dec_ffn_in), Far(dec_ffn_out), Far(dec_gains), Far(dec_biases)],
        [((devices, early_rows, features), BF, "far"), (narrow, BF, "far"), (half, BF), (half, BF),
         (narrow, F32), ((6, features), F32, "far")],
        [bias_scratch, id_scratch, (narrow, BF), all_keys, pair_stats, (narrow, F32), (narrow, BF),
         (narrow, BF), all_keys, ((length, features), BF)],
        28,
    )
    early = lax.psum_scatter(shards, "dp", scatter_dimension=0, tiled=True)[0]
    memory_sum = GroupSum(memory_keep, memory_send, count, devices)
    memory_sum.send()
    memory_sum.finish(order)
    target_keep, target_send, pack_d, dkv_d = order.call(
        decoder_self_back, many,
        [d_target, names, Far(q_d), Far(kv_d), Far(stats_d), Far(mixed_d), Far(dec_self_in),
         Far(dec_self_out)],
        [(half, BF), (half, BF), ((3 * own, features), BF, "far"), (*all_keys, "far")],
        [bias_scratch, id_scratch, (narrow, BF), (narrow, BF)],
        14,
    )
    target_sum = GroupSum(target_keep, target_send, count, devices)
    target_sum.send()
    d_source, vectors_e, send_u, keep_u = order.call(
        encoder_ffn_back, len(memory_sum.arrays),
        [*memory_sum.arrays, Far(norms_e), Far(enc_ffn_in), Far(enc_ffn_out), Far(enc_gains),
         Far(enc_biases)],
        [(narrow, F32), ((4, features), F32, "far"), *bucket(ffn_rows)],
        [product],
        9,
    )
    latter = DpSum(send_u, keep_u, devices)
    latter.step()
    target_sum.finish(order)
    source_keep, source_send, pack_e, dkv_e = order.call(
        encoder_attention_back, many,
        [d_source, names, Far(q_e), Far(kv_e), Far(stats_e), Far(mixed_e), Far(enc_attn_in),
         Far(enc_attn_out)],
        [(half, BF), (half, BF), ((3 * own, features), BF, "far"), (*all_keys, "far")],
        [bias_scratch, id_scratch, (narrow, BF), (narrow, BF)],
        14,
    )
    source_sum = GroupSum(source_keep, source_send, count, devices)
    source_sum.send()
    send_s, keep_s = order.call(
        late_weights, many,
        [*map(Far, source_pieces), target,
         *map(Far, [pack_d, dkv_d, pack_e, dkv_e, vectors_d, vectors_e])],
        bucket(8 * shard + VECTOR_ROWS),
        [small_product, ((length, features), BF)],
        6, [*target_sum.arrays[1:], *latter.parts],
    )
    back = leave(jnp.stack([out_own, first_rows(target_sum.arrays, own).astype(BF)]))
    former = DpSum(send_s, keep_s, devices)
    former.step()
    latter.step()
    early, back, source_sum.arrays, former.parts, latter.parts = fence(
        early, back, source_sum.arrays, former.parts, latter.parts
    )
    early = LineSum(early, count)
    early.step()
    back = lax.all_gather(back, "src", axis=1, tiled=True)
    dec_out, tgt_grad = back[0], back[1]
    while not source_sum.done():
        rows = source_sum.arrays[-1].shape[0] // 2
        source_sum.to_send = first_rows([a[rows:] for a in source_sum.arrays], rows).astype(BF)
        source_sum.send()
    former.step()
    while latter.left:
        latter.step()
    src_grad = leave(first_rows(source_sum.arrays, own).astype(BF))
    early.parts, src_grad, former.parts, latter.parts = fence(
        early.parts, src_grad, former.parts, latter.parts
    )
    early.step()
    latter = LineSum(jnp.concatenate(latter.parts, axis=0), count)
    latter.step()
    while former.left:
        former.step()
    early.parts, latter.parts, former.parts = fence(early.parts, latter.parts, former.parts)
    lines = [LineSum(jnp.concatenate(former.parts, axis=0), count), latter, early]
    while any(line.hop < count - 1 for line in lines):
        for line in lines:
            if line.hop < count - 1:
                line.step()
    selfs, ffn_e, early = (line.parts[0].astype(F32) for line in lines)
    src_grad = src_grad.astype(F32)
    tgt_grad = tgt_grad.astype(F32)
    self_d, attn_e = selfs[: 4 * shard], selfs[4 * shard :]
    ffn_d, cross = early[:ffn_rows], early[ffn_rows:]

    def wide(rows):
        return jnp.concatenate(jnp.split(rows, rows.shape[0] // shard, axis=0), axis=1)

    up = shard * (hidden // features)
    vectors = attn_e[4 * shard :]
    vectors = lax.dynamic_slice_in_dim(vectors, me_dp * shard, shard, 1)
    return (
        dec_out[None],
        src_grad[None],
        tgt_grad[None],
        wide(attn_e[: 3 * shard]),
        attn_e[3 * shard : 4 * shard],
        wide(ffn_e[:up]),
        ffn_e[up:],
        jnp.stack([vectors[8], vectors[6]]),
        jnp.stack([vectors[9], vectors[7]]),
        wide(self_d[: 3 * shard]),
        self_d[3 * shard :],
        cross[shard : 2 * shard],
        wide(cross[2 * shard :]),
        cross[:shard],
        wide(ffn_d[:up]),
        ffn_d[up:],
        jnp.stack([vectors[4], vectors[2], vectors[0]]),
        jnp.stack([vectors[5], vectors[3], vectors[1]]),
    )


def solution(mesh):
    row, part = P("dp", None, None), P("dp", "src", None)
    line, rows, columns = P("dp", None), P("dp", None), P(None, "dp")
    in_specs = (part, line, row, line, row) + (P(),) * 15
    out_specs = (
        row, part, row, rows, rows, rows, rows, columns, columns,
        rows, rows, rows, rows, rows, rows, rows, columns, columns,
    )
    return jax.shard_map(local, mesh=mesh, in_specs=in_specs, out_specs=out_specs, check_vma=False)
```
